32 devices in a mesh: groups: 2 (over y), expert: 4 (over z), dp: 4 (over x, core).
Axes of the slice: x: 2, y: 2, z: 4, core: 2. Of those that a mesh axis runs over, the one named last changes fastest.
Arguments:
- norm_input: bfloat16 [512, 1792], P(('groups', 'expert', 'dp')), parts along dimension 0, may hold values from -6 to 6
- out_grad: bfloat16 [512, 1792], P(('groups', 'expert', 'dp')), parts along dimension 0, may hold values from -6 to 6
- shared_out: bfloat16 [512, 1792], P(('groups', 'expert', 'dp')), parts along dimension 0, may hold values from -1.1953125 to 1.1953125
- expert_ids: int32 [512, 8], P(('groups', 'expert', 'dp')), parts along dimension 0, may hold values from 0 to 63, all different within a row; in each aligned block of 64 rows (0 to 63, 64 to 127, ...) at most 12 rows name the same one
- route_weight: bfloat16 [512, 8], P(('groups', 'expert', 'dp')), parts along dimension 0, may hold values from 0.019897461 to 0.5
- shared_gate: bfloat16 [1792], replicated, may hold values from -0.125 to 0.125
- w_gate: bfloat16 [64, 1792, 1536], P('expert', None, 'dp'), may hold values from -0.125 to 0.125
- w_up: bfloat16 [64, 1792, 1536], P('expert', None, 'dp'), may hold values from -0.125 to 0.125
- w_down: bfloat16 [64, 1536, 1792], P('expert', 'dp'), may hold values from -0.15625 to 0.15625
Outputs:
- input_grad: bfloat16 [512, 1792], P(('groups', 'expert', 'dp')), parts along dimension 0
- route_grad: float32 [512, 8], P(('groups', 'expert', 'dp')), parts along dimension 0
- gate_grad: float32 [3584], P('groups'), parts along dimension 0
The draws below stay inside these ranges and needn't reach their ends.
There are 2 independent parts, one for each index of `groups`. The reference program is written for one: setup_inputs(seed, part) draws one part's arguments, and reference() takes and returns one part's arrays. A program takes and returns all parts, laid end to end along the dimension named above; an argument that names none is the same for every part. Nothing has to cross between parts.
Inputs may be any that keep to these rules, and one draw needn't show every extreme that they name: `expert_ids`: each token names 8 different experts. Tokens come in aligned blocks of 64 (rows 0 to 63, and so on); within a block no expert is named by more than 12 rows, and in some block one expert is named by exactly 12 rows.
All inputs are finite; a program needn't handle non-finite values.
Results may differ from the reference program's by a relative error of at most 0.013.
Values may be sent and summed in bfloat16 or wider, within the bound.
No kernel may reach another device: no remote copies, remote signals or barrier semaphores. Data moves between devices by JAX's collectives and lax.ppermute only.
A program may use at most 192 MiB of HBM per device.

```python
import math
import jax
import jax.numpy as jnp
import numpy as np
from jax import lax

D = 1792
FF_E = 1536
EXPERTS = 64
TOPK = 8
TOK_DEV = 16
CAP = 12
GROUP_TOK = 64
TOKENS = 256
N_DP = 4


def steps_of(own_key, dims, pieces, least, high):
    def one(dim, blocks):
        heights = jax.random.uniform(jax.random.fold_in(jax.random.fold_in(own_key, 6), dim), (blocks,), jnp.float32, least / len(pieces), high / len(pieces))
        return jnp.repeat(jnp.exp(heights), dims[dim] // blocks).reshape((-1,) + (1,) * (len(dims) - dim - 1))

    loudness = one(*pieces[0])
    for cut in pieces[1:]:
        loudness = loudness * one(*cut)
    return loudness


def assign_block(key, own, number, rows, number_of, top, most, skew):
    sequence = jax.random.permutation(key, number_of)
    crowded, ordinary = portions_of(number_of, rows * top, most, skew, True), portions_of(number_of, rows * top, most, skew, False)
    places = jnp.arange(number_of)

    def named(sizes, turn):
        used = int((sizes > 0).sum())
        fixed = max(1, used // 4)
        moved = fixed + (places - fixed + turn * (used - fixed)) % max(1, number_of - fixed)
        return jnp.zeros((number_of,), jnp.int32).at[sequence[jnp.where(places < fixed, places, moved)]].set(jnp.asarray(sizes, jnp.int32))

    sizes = jnp.where(number % 4 == 0, named(crowded, number // 4), named(ordinary, number - number // 4 - 1))
    mixed = jax.random.permutation(jax.random.fold_in(own, 3), number_of)
    donor, receiver = mixed[0:number_of // 2 * 2:2], mixed[1:number_of // 2 * 2:2]
    room = jnp.minimum(sizes[donor] - 1, most - sizes[receiver]) // 2
    room = jnp.where((donor == sequence[0]) | (receiver == sequence[0]) | (sizes[receiver] == 0), 0, jnp.maximum(room, 0))
    moved = jax.random.randint(jax.random.fold_in(own, 4), (number_of // 2,), 0, 1 << 20) % (room + 1)
    sizes = sizes.at[donor].add(-moved).at[receiver].add(moved)
    labels = jnp.searchsorted(jnp.cumsum(sizes), jnp.arange(rows * top), side="right").astype(jnp.int32)
    grid = labels.reshape(top, rows).T
    grid = grid[jax.random.permutation(jax.random.fold_in(own, 1), rows)]
    turn = jax.random.randint(jax.random.fold_in(own, 2), (rows, 1), 0, top)
    return jnp.take_along_axis(grid, (jnp.arange(top)[None, :] + turn) % top, axis=1)


def portions_of(number_of, total, limit, slope, full):
    portions = [(1 << 20) // math.isqrt(standing ** slope) + 1 for standing in range(1, number_of + 1)]
    largest = limit if full else min(limit, max(-(-total // number_of), total * portions[0] // sum(portions)))
    least = 1 if total - largest >= number_of - 1 else 0
    given, rest = [largest] + [least] * (number_of - 1), total - largest - least * (number_of - 1)
    while rest > 0:
        free = [i for i in range(1, number_of) if given[i] < largest] or [i for i in range(1, number_of) if given[i] < limit]
        pool, left = sum([portions[i] for i in free]), rest
        for i in free:
            addition = min(limit - given[i], max(1, left * portions[i] // pool), rest)
            given[i] = given[i] + addition
            rest = rest - addition
    return np.array(given)


def bell_draw(own_key, shape, spread, limit, cuts=(), kind=jnp.bfloat16):
    drawn = spread * jax.random.normal(own_key, shape, jnp.float32)
    if cuts:
        drawn = drawn * steps_of(own_key, shape, cuts, -0.22, 0.18)
    return jnp.clip(drawn, -limit, limit).astype(kind)


def setup_inputs(seed: int = 0, part: int = 0) -> dict:
    seeds = jax.random.split(jax.random.key(seed), 10)
    own_keys = jax.random.split(jax.random.fold_in(seeds[9], part), 10)
    norm_input = bell_draw(own_keys[0], (TOKENS, D), 1.0, 6.0, ((0, 16),))
    out_grad = bell_draw(own_keys[1], (TOKENS, D), 1.0, 6.0, ((0, 16),))
    shared_out = bell_draw(own_keys[2], (TOKENS, D), 0.2, 1.1953125, ((0, 16),))
    expert_ids_keys = jax.random.split(jax.random.fold_in(own_keys[3], 1), TOKENS // GROUP_TOK)
    expert_ids_turns = jax.random.permutation(jax.random.fold_in(own_keys[3], 3), TOKENS // GROUP_TOK)
    expert_ids = jax.vmap(lambda own, number: assign_block(jax.random.fold_in(own_keys[3], 2), own, number, GROUP_TOK, EXPERTS, TOPK, CAP, 2))(expert_ids_keys, expert_ids_turns).reshape((TOKENS, TOPK))
    route_weight = jnp.clip(jnp.exp(math.log(0.5) - 3.224016 * jax.random.uniform(own_keys[4], (TOKENS, TOPK), jnp.float32) ** steps_of(own_keys[4], (TOKENS, TOPK), ((0, 16),), -0.2, 0.2)), 0.019897461, 0.5).astype(jnp.bfloat16)
    shared_gate = bell_draw(seeds[5], (D,), D ** -0.5, 0.125)
    w_gate = bell_draw(seeds[6], (EXPERTS, D, FF_E), D ** -0.5, 0.125, ((0, 4), (2, 4)))
    w_up = bell_draw(seeds[7], (EXPERTS, D, FF_E), D ** -0.5, 0.125, ((0, 4), (2, 4)))
    w_down = bell_draw(seeds[8], (EXPERTS, FF_E, D), FF_E ** -0.5, 0.15625, ((0, 4), (1, 4)))
    return dict(norm_input=norm_input, out_grad=out_grad, shared_out=shared_out, expert_ids=expert_ids, route_weight=route_weight, shared_gate=shared_gate, w_gate=w_gate, w_up=w_up, w_down=w_down)


def slot_targets(group_ids):
    flat_ids = group_ids.reshape(-1).astype(jnp.int32)
    one_hot = (flat_ids[:, None] == jnp.arange(EXPERTS, dtype=jnp.int32)[None, :]).astype(jnp.int32)
    before = jnp.cumsum(one_hot, axis=0) - one_hot
    position = jnp.sum(before * one_hot, axis=1).astype(jnp.int32)
    return (flat_ids * CAP + position).astype(jnp.int32)


def dispatch_matrix(target, group_tokens):
    slots = jnp.arange(EXPERTS * CAP, dtype=jnp.int32)
    hits = (target[None, :] == slots[:, None]).astype(jnp.float32)
    return hits.reshape(EXPERTS * CAP, group_tokens, TOPK).sum(axis=2)


def reference(norm_input, out_grad, shared_out, expert_ids, route_weight, shared_gate, w_gate, w_up, w_down):
    group_tokens = TOK_DEV * N_DP
    group_count = TOKENS // group_tokens
    block_size = FF_E // N_DP
    gate_full = w_gate.astype(jnp.float32)
    up_full = w_up.astype(jnp.float32)
    down_full = w_down.astype(jnp.float32)
    gate_blocks = gate_full.reshape(EXPERTS, D, N_DP, block_size)
    up_blocks = up_full.reshape(EXPERTS, D, N_DP, block_size)

    def one_group(inputs):
        group_norm, group_grad, group_ids, group_weight = inputs
        target = slot_targets(group_ids)
        dispatch = dispatch_matrix(target, group_tokens)
        slot_norm = jnp.dot(dispatch, group_norm.astype(jnp.float32)).reshape(EXPERTS, CAP, D)
        slot_grad = jnp.dot(dispatch, group_grad.astype(jnp.float32)).reshape(EXPERTS, CAP, D)
        gate_pre = jnp.einsum('ecd,edf->ecf', slot_norm, gate_full)
        up_pre = jnp.einsum('ecd,edf->ecf', slot_norm, up_full)
        hidden_grad = jnp.einsum('ecd,efd->ecf', slot_grad, down_full)
        logistic = jax.nn.sigmoid(gate_pre)
        swish = gate_pre * logistic
        act = swish * up_pre
        gate_diff = (hidden_grad * up_pre * logistic * (1.0 + gate_pre * (1.0 - logistic))).astype(jnp.bfloat16)
        up_diff = (hidden_grad * swish).astype(jnp.bfloat16)
        gate_diff = lax.optimization_barrier(gate_diff).astype(jnp.float32).reshape(EXPERTS, CAP, N_DP, block_size)
        up_diff = lax.optimization_barrier(up_diff).astype(jnp.float32).reshape(EXPERTS, CAP, N_DP, block_size)
        row_part = jnp.einsum('ecpf,edpf->ecpd', gate_diff, gate_blocks) + jnp.einsum('ecpf,edpf->ecpd', up_diff, up_blocks)
        row_part = lax.optimization_barrier(row_part.astype(jnp.bfloat16)).astype(jnp.float32)
        row_sum = jnp.sum(row_part, axis=2).reshape(EXPERTS * CAP, D)
        score_part = jnp.sum((act * hidden_grad).reshape(EXPERTS, CAP, N_DP, block_size), axis=3)
        score_part = lax.optimization_barrier(score_part.astype(jnp.bfloat16)).astype(jnp.float32)
        score_sum = jnp.sum(score_part, axis=2).reshape(EXPERTS * CAP)
        picked = row_sum[target].reshape(group_tokens, TOPK, D)
        routed = jnp.einsum('tk,tkd->td', group_weight.astype(jnp.float32), picked)
        scores = score_sum[target].reshape(group_tokens, TOPK)
        return routed, scores

    routed, route_grad = lax.map(one_group, (
        norm_input.reshape(group_count, group_tokens, D),
        out_grad.reshape(group_count, group_tokens, D),
        expert_ids.reshape(group_count, group_tokens, TOPK),
        route_weight.reshape(group_count, group_tokens, TOPK)))
    routed = routed.reshape(TOKENS, D)
    route_grad = route_grad.reshape(TOKENS, TOPK)
    gate_value = jax.nn.sigmoid(jnp.dot(norm_input, shared_gate, preferred_element_type=jnp.float32))
    inner = jnp.sum(out_grad.astype(jnp.float32) * shared_out.astype(jnp.float32), axis=1)
    gate_delta = inner * gate_value * (1.0 - gate_value)
    input_grad = (routed + gate_delta[:, None] * shared_gate.astype(jnp.float32)[None, :]).astype(jnp.bfloat16)
    gate_grad = jnp.dot(gate_delta, norm_input.astype(jnp.float32), precision=lax.Precision.HIGHEST)
    return input_grad, route_grad, gate_grad
```

```python
import functools

import jax
import jax.numpy as jnp
from jax import lax
from jax.experimental import pallas as pl
from jax.experimental.pallas import tpu as pltpu
from jax.sharding import PartitionSpec as P

EXPERTS = 64
TOPK = 8
CAP = 12
LANES = 128
BF16 = jnp.bfloat16
F32 = jnp.float32
NT = (((1,), (1,)), ((), ()))
TN = (((0,), (0,)), ((), ()))


def slot_targets(group_ids):
    flat_ids = group_ids.reshape(-1)
    one_hot = (flat_ids[:, None] == jnp.arange(EXPERTS, dtype=jnp.int32)[None, :]).astype(jnp.int32)
    before = jnp.cumsum(one_hot, axis=0) - one_hot
    position = jnp.sum(before * one_hot, axis=1)
    return flat_ids * CAP + position


def general_device(
    norm_input, out_grad, shared_out, expert_ids, route_weight, shared_gate, w_gate, w_up, w_down
):
    features = norm_input.shape[1]
    group_norm, group_grad, group_codes, group_weight = (
        lax.all_gather(norm_input, "dp", axis=0, tiled=True),
        lax.all_gather(out_grad, "dp", axis=0, tiled=True),
        lax.all_gather(expert_ids.astype(jnp.bfloat16), "dp", axis=0, tiled=True),
        lax.all_gather(route_weight, "dp", axis=0, tiled=True),
    )
    group_ids = group_codes.astype(jnp.int32)
    group_tokens = group_norm.shape[0]
    target = slot_targets(group_ids)
    slots = jnp.arange(EXPERTS * CAP, dtype=jnp.int32)
    hits = (target[None, :] == slots[:, None]).astype(jnp.bfloat16)
    dispatch = hits.reshape(EXPERTS * CAP, group_tokens, TOPK).sum(axis=2)
    slot_norm = jnp.dot(dispatch, group_norm, preferred_element_type=jnp.float32).astype(
        jnp.bfloat16
    )
    slot_grad = jnp.dot(dispatch, group_grad, preferred_element_type=jnp.float32).astype(
        jnp.bfloat16
    )
    slot_norm = slot_norm.reshape(EXPERTS, CAP, features)
    slot_grad = slot_grad.reshape(EXPERTS, CAP, features)
    local_experts = w_gate.shape[0]
    quarter = CAP // lax.axis_size("dp")
    offset = lax.axis_index("dp") * quarter
    norm_share = lax.dynamic_slice_in_dim(slot_norm, offset, quarter, 1)
    grad_share = lax.dynamic_slice_in_dim(slot_grad, offset, quarter, 1)
    arrived_norm, arrived_grad = (
        lax.all_to_all(norm_share, "expert", split_axis=0, concat_axis=0, tiled=True),
        lax.all_to_all(grad_share, "expert", split_axis=0, concat_axis=0, tiled=True),
    )
    rows_in = lax.all_gather(arrived_norm, "dp", axis=1, tiled=True)
    grads_in = lax.all_gather(arrived_grad, "dp", axis=1, tiled=True)
    item_count = rows_in.shape[1]
    sources = rows_in.shape[0] // local_experts
    rows_four = rows_in.reshape(sources, local_experts, item_count, features)
    grads_four = grads_in.reshape(sources, local_experts, item_count, features)
    gate_pre = jnp.einsum("sxcd,xdf->sxcf", rows_four, w_gate, preferred_element_type=jnp.float32)
    up_pre = jnp.einsum("sxcd,xdf->sxcf", rows_four, w_up, preferred_element_type=jnp.float32)
    hidden_grad = jnp.einsum(
        "sxcd,xfd->sxcf", grads_four, w_down, preferred_element_type=jnp.float32
    )
    logistic = jax.nn.sigmoid(gate_pre)
    swish = gate_pre * logistic
    act = swish * up_pre
    gate_diff = (hidden_grad * up_pre * logistic * (1.0 + gate_pre * (1.0 - logistic))).astype(
        jnp.bfloat16
    )
    up_diff = (hidden_grad * swish).astype(jnp.bfloat16)
    row_part = jnp.einsum("sxcf,xdf->sxcd", gate_diff, w_gate, preferred_element_type=jnp.float32)
    row_part = row_part + jnp.einsum(
        "sxcf,xdf->sxcd", up_diff, w_up, preferred_element_type=jnp.float32
    )
    row_back = row_part.astype(jnp.bfloat16).reshape(sources * local_experts, item_count, features)
    score_back = jnp.sum(act * hidden_grad, axis=3).astype(jnp.bfloat16)
    score_back = score_back.reshape(sources * local_experts, item_count, 1)
    back_rows = lax.all_to_all(row_back, "expert", split_axis=0, concat_axis=0, tiled=True)
    back_scores = lax.all_to_all(score_back, "expert", split_axis=0, concat_axis=0, tiled=True)
    columns = back_rows.shape[2]
    back_flat = back_rows.reshape(EXPERTS * CAP, columns)
    score_flat = back_scores.reshape(EXPERTS * CAP)
    picked = jnp.take(back_flat, target, axis=0).reshape(group_tokens, TOPK, columns)
    token_part = jnp.einsum(
        "tk,tkd->td", group_weight.astype(jnp.float32), picked.astype(jnp.float32)
    )
    score_part = (
        jnp.take(score_flat, target, axis=0).astype(jnp.float32).reshape(group_tokens, TOPK)
    )
    routed, route_grad = (
        lax.psum_scatter(
            token_part.astype(jnp.bfloat16), "dp", scatter_dimension=0, tiled=True
        ).astype(jnp.float32),
        lax.psum_scatter(
            score_part.astype(jnp.bfloat16), "dp", scatter_dimension=0, tiled=True
        ).astype(jnp.float32),
    )
    gate_value = jax.nn.sigmoid(
        jnp.dot(norm_input, shared_gate, preferred_element_type=jnp.float32)
    )
    inner = jnp.sum(out_grad.astype(jnp.float32) * shared_out.astype(jnp.float32), axis=1)
    gate_delta = inner * gate_value * (1.0 - gate_value)
    input_grad = (routed + gate_delta[:, None] * shared_gate.astype(jnp.float32)[None, :]).astype(
        jnp.bfloat16
    )
    gate_local = jnp.dot(
        gate_delta, norm_input.astype(jnp.float32), precision=lax.Precision.HIGHEST
    )
    gate_grad = lax.psum(gate_local, ("expert", "dp"))
    return (input_grad, route_grad, gate_grad)


def dot(a, b, dims=(((1,), (0,)), ((), ()))):
    return lax.dot_general(a, b, dims, preferred_element_type=F32)


def swap(value, axis, distance):
    size = lax.axis_size(axis)
    return lax.ppermute(value, axis, [(i, i ^ distance) for i in range(size)])


def experts_kernel(features, rows, blocks, *refs):
    token_refs, refs = refs[:blocks], refs[blocks:]
    tail_ref, w_gate, w_up, w_down, keep_ref, send_ref, tokens, copied, spread, weighted, norms, grads, backs, hits, routes = refs
    step, steps = pl.program_id(0), pl.num_programs(0)
    each = token_refs[0].shape[0]
    count = each * blocks

    @pl.when(step == 0)
    def _():
        copies = [
            pltpu.make_async_copy(ref, tokens.at[pl.ds(j * each, each)], copied.at[j])
            for j, ref in enumerate(token_refs)
        ]
        for copy in copies:
            copy.start()
        for copy in copies:
            copy.wait()
        codes = tokens[:, 2 * features :].astype(F32).T
        named = codes[:TOPK]
        weights = codes[TOPK : 2 * TOPK]
        first = (lax.axis_index("expert") * steps).astype(F32)
        hits[...] = named - first
        local = named - first
        earlier = (
            lax.broadcasted_iota(jnp.int32, (count, count), 0)
            < lax.broadcasted_iota(jnp.int32, (count, count), 1)
        ).astype(BF16)
        number = spread.shape[0] // rows
        masks = [local == float(e) for e in range(number)]
        member = jnp.concatenate(
            [jnp.sum(m.astype(F32), axis=0, keepdims=True) for m in masks], axis=0
        )
        position = dot(member.astype(BF16), earlier)
        slot = lax.broadcasted_iota(jnp.int32, (rows, count), 0).astype(F32)
        for e in range(number):
            weight = jnp.sum(jnp.where(masks[e], weights, 0.0), axis=0, keepdims=True)
            chosen = (slot == position[e : e + 1]) & (member[e : e + 1] > 0.0)
            spread[e * rows : (e + 1) * rows] = jnp.where(chosen, 1.0, 0.0).astype(BF16)
            weighted[e * rows : (e + 1) * rows] = jnp.where(chosen, weight, 0.0).astype(BF16)
        norms[...] = dot(spread[...], tokens[:, :features]).astype(BF16)
        grads[...] = dot(spread[...], tokens[:, features : 2 * features]).astype(BF16)
        routes[...] = jnp.zeros_like(routes)

    here = pl.ds(pl.multiple_of(step * rows, rows), rows)
    x, dy = norms[here], grads[here]
    gate_pre = dot(x, w_gate[0])
    up_pre = dot(x, w_up[0])
    hidden_grad = dot(dy, w_down[0], NT)
    logistic = jax.nn.sigmoid(gate_pre)
    swish = gate_pre * logistic
    gate_diff = (hidden_grad * up_pre * logistic * (1.0 + gate_pre * (1.0 - logistic))).astype(BF16)
    up_diff = (hidden_grad * swish).astype(BF16)
    backs[here] = (dot(gate_diff, w_gate[0], NT) + dot(up_diff, w_up[0], NT)).astype(BF16)
    score = jnp.sum(swish * up_pre * hidden_grad, axis=1, keepdims=True)
    by_token = jnp.sum(spread[here].astype(F32) * score, axis=0, keepdims=True)
    routes[...] += jnp.where(hits[...] == step.astype(F32), by_token, 0.0)

    @pl.when(step == steps - 1)
    def _():
        half = count // 2
        result = dot(weighted[...], backs[...], TN).astype(BF16)
        scores = jnp.concatenate([routes[...], jnp.zeros((LANES - TOPK, count), F32)], axis=0).T
        tail = jnp.concatenate([tail_ref[...]] * blocks, axis=0)
        last = (scores + tail).astype(BF16)
        keep_ref[:, :features] = result[:half]
        send_ref[:, :features] = result[half:]
        keep_ref[:, features:] = last[:half]
        send_ref[:, features:] = last[half:]


def run_experts(token_blocks, tail, w_gate, w_up, w_down, sources):
    local, features, hidden = w_gate.shape
    blocks = len(token_blocks)
    count = blocks * token_blocks[0].shape[0]
    rows = sources * CAP
    width = features + LANES
    return pl.pallas_call(
        functools.partial(experts_kernel, features, rows, blocks),
        grid=(local,),
        in_specs=[pl.BlockSpec(memory_space=pl.ANY)] * blocks
        + [
            pl.BlockSpec(tail.shape, lambda i: (0, 0)),
            pl.BlockSpec((1, features, hidden), lambda i: (i, 0, 0)),
            pl.BlockSpec((1, features, hidden), lambda i: (i, 0, 0)),
            pl.BlockSpec((1, hidden, features), lambda i: (i, 0, 0)),
        ],
        out_specs=[pl.BlockSpec((count // 2, width), lambda i: (0, 0))] * 2,
        out_shape=[jax.ShapeDtypeStruct((count // 2, width), BF16)] * 2,
        scratch_shapes=[
            pltpu.VMEM((count, 2 * features + LANES), BF16),
            pltpu.SemaphoreType.DMA((blocks,)),
            pltpu.VMEM((local * rows, count), BF16),
            pltpu.VMEM((local * rows, count), BF16),
            pltpu.VMEM((local * rows, features), BF16),
            pltpu.VMEM((local * rows, features), BF16),
            pltpu.VMEM((local * rows, features), BF16),
            pltpu.VMEM((TOPK, count), F32),
            pltpu.VMEM((TOPK, count), F32),
        ],
        compiler_params=pltpu.CompilerParams(vmem_limit_bytes=48 << 20),
        name="experts",
    )(*token_blocks, tail, w_gate, w_up, w_down)


def square_device(
    norm_input, out_grad, shared_out, expert_ids, route_weight, shared_gate, w_gate, w_up, w_down
):
    tokens, features = norm_input.shape
    sources = lax.axis_size("expert")
    codes = jnp.concatenate(
        [
            expert_ids.astype(BF16),
            route_weight,
            jnp.zeros((tokens, LANES - 2 * TOPK), BF16),
        ],
        axis=1,
    )
    mine = jnp.concatenate([norm_input, out_grad, codes], axis=1)
    held = [mine] + [swap(mine, "expert", d) for d in range(1, sources)]
    held = held + [swap(block, "dp", 2) for block in held]
    held = held + [swap(block, "dp", 1) for block in held]

    gate_value = jax.nn.sigmoid(
        jnp.dot(norm_input, shared_gate, preferred_element_type=F32)
    )
    inner = jnp.sum(out_grad.astype(F32) * shared_out.astype(F32), axis=1)
    gate_delta = inner * gate_value * (1.0 - gate_value)
    gate_local = jnp.sum(gate_delta[:, None] * norm_input.astype(F32), axis=0)
    share = features // tokens
    tail = jnp.pad(gate_local.reshape(tokens, share), ((0, 0), (TOPK, LANES - TOPK - share)))

    kept, sent = run_experts(held, tail, w_gate, w_up, w_down, sources)
    total = (kept.astype(F32) + swap(sent, "dp", 1).astype(F32)).astype(BF16)
    half = total.shape[0] // 2
    total = (total[:half].astype(F32) + swap(total[half:], "dp", 2).astype(F32)).astype(BF16)
    final = total[:tokens].astype(F32)
    for d in range(1, sources):
        final = final + swap(total[d * tokens : (d + 1) * tokens], "expert", d).astype(F32)
    input_grad = (
        final[:, :features] + gate_delta[:, None] * shared_gate.astype(F32)[None, :]
    ).astype(BF16)
    route_grad = final[:, features : features + TOPK]
    gate_grad = final[:, features + TOPK : features + TOPK + share].reshape(features)
    return (input_grad, route_grad, gate_grad)


def solution(mesh):
    square = mesh.shape["expert"] == 4 and mesh.shape["dp"] == 4
    on_device = square_device if square else general_device
    return jax.shard_map(
        on_device,
        mesh=mesh,
        in_specs=(
            P(("groups", "expert", "dp"), None),
            P(("groups", "expert", "dp"), None),
            P(("groups", "expert", "dp"), None),
            P(("groups", "expert", "dp"), None),
            P(("groups", "expert", "dp"), None),
            P(),
            P("expert", None, "dp"),
            P("expert", None, "dp"),
            P("expert", "dp", None),
        ),
        out_specs=(
            P(("groups", "expert", "dp"), None),
            P(("groups", "expert", "dp"), None),
            P("groups"),
        ),
        check_vma=False,
    )
```

```python
import functools

import jax
import jax.numpy as jnp
from jax import lax
from jax.experimental import pallas as pl
from jax.experimental.pallas import tpu as pltpu
from jax.sharding import PartitionSpec as P

EXPERTS = 64
TOPK = 8
CAP = 12
LANES = 128
BF16 = jnp.bfloat16
F32 = jnp.float32
NT = (((1,), (1,)), ((), ()))
TN = (((0,), (0,)), ((), ()))


def slot_targets(group_ids):
    flat_ids = group_ids.reshape(-1)
    one_hot = (flat_ids[:, None] == jnp.arange(EXPERTS, dtype=jnp.int32)[None, :]).astype(jnp.int32)
    before = jnp.cumsum(one_hot, axis=0) - one_hot
    position = jnp.sum(before * one_hot, axis=1)
    return flat_ids * CAP + position


def general_device(
    norm_input, out_grad, shared_out, expert_ids, route_weight, shared_gate, w_gate, w_up, w_down
):
    features = norm_input.shape[1]
    group_norm, group_grad, group_codes, group_weight = (
        lax.all_gather(norm_input, "dp", axis=0, tiled=True),
        lax.all_gather(out_grad, "dp", axis=0, tiled=True),
        lax.all_gather(expert_ids.astype(jnp.bfloat16), "dp", axis=0, tiled=True),
        lax.all_gather(route_weight, "dp", axis=0, tiled=True),
    )
    group_ids = group_codes.astype(jnp.int32)
    group_tokens = group_norm.shape[0]
    target = slot_targets(group_ids)
    slots = jnp.arange(EXPERTS * CAP, dtype=jnp.int32)
    hits = (target[None, :] == slots[:, None]).astype(jnp.bfloat16)
    dispatch = hits.reshape(EXPERTS * CAP, group_tokens, TOPK).sum(axis=2)
    slot_norm = jnp.dot(dispatch, group_norm, preferred_element_type=jnp.float32).astype(
        jnp.bfloat16
    )
    slot_grad = jnp.dot(dispatch, group_grad, preferred_element_type=jnp.float32).astype(
        jnp.bfloat16
    )
    slot_norm = slot_norm.reshape(EXPERTS, CAP, features)
    slot_grad = slot_grad.reshape(EXPERTS, CAP, features)
    local_experts = w_gate.shape[0]
    quarter = CAP // lax.axis_size("dp")
    offset = lax.axis_index("dp") * quarter
    norm_share = lax.dynamic_slice_in_dim(slot_norm, offset, quarter, 1)
    grad_share = lax.dynamic_slice_in_dim(slot_grad, offset, quarter, 1)
    arrived_norm, arrived_grad = (
        lax.all_to_all(norm_share, "expert", split_axis=0, concat_axis=0, tiled=True),
        lax.all_to_all(grad_share, "expert", split_axis=0, concat_axis=0, tiled=True),
    )
    rows_in = lax.all_gather(arrived_norm, "dp", axis=1, tiled=True)
    grads_in = lax.all_gather(arrived_grad, "dp", axis=1, tiled=True)
    item_count = rows_in.shape[1]
    sources = rows_in.shape[0] // local_experts
    rows_four = rows_in.reshape(sources, local_experts, item_count, features)
    grads_four = grads_in.reshape(sources, local_experts, item_count, features)
    gate_pre = jnp.einsum("sxcd,xdf->sxcf", rows_four, w_gate, preferred_element_type=jnp.float32)
    up_pre = jnp.einsum("sxcd,xdf->sxcf", rows_four, w_up, preferred_element_type=jnp.float32)
    hidden_grad = jnp.einsum(
        "sxcd,xfd->sxcf", grads_four, w_down, preferred_element_type=jnp.float32
    )
    logistic = jax.nn.sigmoid(gate_pre)
    swish = gate_pre * logistic
    act = swish * up_pre
    gate_diff = (hidden_grad * up_pre * logistic * (1.0 + gate_pre * (1.0 - logistic))).astype(
        jnp.bfloat16
    )
    up_diff = (hidden_grad * swish).astype(jnp.bfloat16)
    row_part = jnp.einsum("sxcf,xdf->sxcd", gate_diff, w_gate, preferred_element_type=jnp.float32)
    row_part = row_part + jnp.einsum(
        "sxcf,xdf->sxcd", up_diff, w_up, preferred_element_type=jnp.float32
    )
    row_back = row_part.astype(jnp.bfloat16).reshape(sources * local_experts, item_count, features)
    score_back = jnp.sum(act * hidden_grad, axis=3).astype(jnp.bfloat16)
    score_back = score_back.reshape(sources * local_experts, item_count, 1)
    back_rows = lax.all_to_all(row_back, "expert", split_axis=0, concat_axis=0, tiled=True)
    back_scores = lax.all_to_all(score_back, "expert", split_axis=0, concat_axis=0, tiled=True)
    columns = back_rows.shape[2]
    back_flat = back_rows.reshape(EXPERTS * CAP, columns)
    score_flat = back_scores.reshape(EXPERTS * CAP)
    picked = jnp.take(back_flat, target, axis=0).reshape(group_tokens, TOPK, columns)
    token_part = jnp.einsum(
        "tk,tkd->td", group_weight.astype(jnp.float32), picked.astype(jnp.float32)
    )
    score_part = (
        jnp.take(score_flat, target, axis=0).astype(jnp.float32).reshape(group_tokens, TOPK)
    )
    routed, route_grad = (
        lax.psum_scatter(
            token_part.astype(jnp.bfloat16), "dp", scatter_dimension=0, tiled=True
        ).astype(jnp.float32),
        lax.psum_scatter(
            score_part.astype(jnp.bfloat16), "dp", scatter_dimension=0, tiled=True
        ).astype(jnp.float32),
    )
    gate_value = jax.nn.sigmoid(
        jnp.dot(norm_input, shared_gate, preferred_element_type=jnp.float32)
    )
    inner = jnp.sum(out_grad.astype(jnp.float32) * shared_out.astype(jnp.float32), axis=1)
    gate_delta = inner * gate_value * (1.0 - gate_value)
    input_grad = (routed + gate_delta[:, None] * shared_gate.astype(jnp.float32)[None, :]).astype(
        jnp.bfloat16
    )
    gate_local = jnp.dot(
        gate_delta, norm_input.astype(jnp.float32), precision=lax.Precision.HIGHEST
    )
    gate_grad = lax.psum(gate_local, ("expert", "dp"))
    return (input_grad, route_grad, gate_grad)


def dot(a, b, dims=(((1,), (0,)), ((), ()))):
    return lax.dot_general(a, b, dims, preferred_element_type=F32)


def swap(value, axis, distance):
    size = lax.axis_size(axis)
    return lax.ppermute(value, axis, [(i, i ^ distance) for i in range(size)])


def experts_kernel(features, rows, blocks, group, *refs):
    token_refs, refs = refs[:blocks], refs[blocks:]
    tail_ref, w_gate, w_up, w_down, keep_ref, send_ref, tokens, copied, gates, ups, downs, loaded, spread, weighted, norms, grads, backs, hits, routes = refs
    number = w_gate.shape[0]
    each = token_refs[0].shape[0]
    count = each * blocks

    def loads(turn, k):
        expert = turn * group + k
        slot = lax.rem(turn, 2) * group + k
        return [
            pltpu.make_async_copy(source.at[expert], target.at[slot], loaded.at[slot, j])
            for j, (source, target) in enumerate(((w_gate, gates), (w_up, ups), (w_down, downs)))
        ]

    copies = [
        pltpu.make_async_copy(ref, tokens.at[pl.ds(j * each, each)], copied.at[j])
        for j, ref in enumerate(token_refs)
    ]
    for copy in copies:
        copy.start()
    for turn in range(2):
        for k in range(group):
            for copy in loads(turn, k):
                copy.start()
    for copy in copies:
        copy.wait()
    codes = tokens[:, 2 * features :].astype(F32).T
    weights = codes[TOPK : 2 * TOPK]
    local = codes[:TOPK] - (lax.axis_index("expert") * number).astype(F32)
    hits[...] = local
    earlier = (
        lax.broadcasted_iota(jnp.int32, (count, count), 0)
        < lax.broadcasted_iota(jnp.int32, (count, count), 1)
    ).astype(BF16)
    masks = [local == float(e) for e in range(number)]
    member = jnp.concatenate(
        [jnp.sum(m.astype(F32), axis=0, keepdims=True) for m in masks], axis=0
    )
    position = dot(member.astype(BF16), earlier)
    slot = lax.broadcasted_iota(jnp.int32, (rows, count), 0).astype(F32)
    for e in range(number):
        weight = jnp.sum(jnp.where(masks[e], weights, 0.0), axis=0, keepdims=True)
        chosen = (slot == position[e : e + 1]) & (member[e : e + 1] > 0.0)
        spread[e * rows : (e + 1) * rows] = jnp.where(chosen, 1.0, 0.0).astype(BF16)
        weighted[e * rows : (e + 1) * rows] = jnp.where(chosen, weight, 0.0).astype(BF16)
    norms[...] = dot(spread[...], tokens[:, :features]).astype(BF16)
    grads[...] = dot(spread[...], tokens[:, features : 2 * features]).astype(BF16)
    routes[...] = jnp.zeros_like(routes)

    def run(turn, _):
        base = lax.rem(turn, 2) * group
        heres = [
            pl.ds(pl.multiple_of((turn * group + k) * rows, rows), rows) for k in range(group)
        ]
        for k in range(group):
            for copy in loads(turn, k):
                copy.wait()
        pre = []
        for k in range(group):
            x, dy = norms[heres[k]], grads[heres[k]]
            pre.append((dot(x, gates[base + k]), dot(x, ups[base + k]), dot(dy, downs[base + k], NT)))
        for k in range(group):
            gate_pre, up_pre, hidden_grad = pre[k]
            logistic = jax.nn.sigmoid(gate_pre)
            swish = gate_pre * logistic
            gate_diff = (
                hidden_grad * up_pre * logistic * (1.0 + gate_pre * (1.0 - logistic))
            ).astype(BF16)
            up_diff = (hidden_grad * swish).astype(BF16)
            first_part = dot(gate_diff, gates[base + k], NT)
            second_part = dot(ups[base + k], up_diff, NT).T
            backs[heres[k]] = (first_part + second_part).astype(BF16)
            score = jnp.sum(swish * up_pre * hidden_grad, axis=1, keepdims=True)
            by_token = jnp.sum(spread[heres[k]].astype(F32) * score, axis=0, keepdims=True)
            here = (turn * group + k).astype(F32)
            routes[...] += jnp.where(hits[...] == here, by_token, 0.0)

        @pl.when(turn + 2 < number // group)
        def _():
            for k in range(group):
                for copy in loads(turn + 2, k):
                    copy.start()

        return 0

    lax.fori_loop(0, number // group, run, 0)
    half = count // 2
    result = dot(weighted[...], backs[...], TN).astype(BF16)
    scores = jnp.concatenate([routes[...], jnp.zeros((LANES - TOPK, count), F32)], axis=0).T
    tail = jnp.concatenate([tail_ref[...]] * blocks, axis=0)
    last = (scores + tail).astype(BF16)
    keep_ref[:, :features] = result[:half]
    send_ref[:, :features] = result[half:]
    keep_ref[:, features:] = last[:half]
    send_ref[:, features:] = last[half:]


def run_experts(token_blocks, tail, w_gate, w_up, w_down, sources):
    local, features, hidden = w_gate.shape
    blocks = len(token_blocks)
    count = blocks * token_blocks[0].shape[0]
    rows = sources * CAP
    width = features + LANES
    group = 2
    away = pl.BlockSpec(memory_space=pl.ANY)
    near = pl.BlockSpec(memory_space=pltpu.VMEM)
    return pl.pallas_call(
        functools.partial(experts_kernel, features, rows, blocks, group),
        in_specs=[away] * blocks + [near, away, away, away],
        out_specs=[near] * 2,
        out_shape=[jax.ShapeDtypeStruct((count // 2, width), BF16)] * 2,
        scratch_shapes=[
            pltpu.VMEM((count, 2 * features + LANES), BF16),
            pltpu.SemaphoreType.DMA((blocks,)),
            pltpu.VMEM((2 * group, features, hidden), BF16),
            pltpu.VMEM((2 * group, features, hidden), BF16),
            pltpu.VMEM((2 * group, hidden, features), BF16),
            pltpu.SemaphoreType.DMA((2 * group, 3)),
            pltpu.VMEM((local * rows, count), BF16),
            pltpu.VMEM((local * rows, count), BF16),
            pltpu.VMEM((local * rows, features), BF16),
            pltpu.VMEM((local * rows, features), BF16),
            pltpu.VMEM((local * rows, features), BF16),
            pltpu.VMEM((TOPK, count), F32),
            pltpu.VMEM((TOPK, count), F32),
        ],
        compiler_params=pltpu.CompilerParams(vmem_limit_bytes=60 << 20),
        name="experts",
    )(*token_blocks, tail, w_gate, w_up, w_down)


def square_device(
    norm_input, out_grad, shared_out, expert_ids, route_weight, shared_gate, w_gate, w_up, w_down
):
    tokens, features = norm_input.shape
    sources = lax.axis_size("expert")
    codes = jnp.concatenate(
        [
            expert_ids.astype(BF16),
            route_weight,
            jnp.zeros((tokens, LANES - 2 * TOPK), BF16),
        ],
        axis=1,
    )
    mine = jnp.concatenate([norm_input, out_grad, codes], axis=1)
    held = [mine] + [swap(mine, "expert", d) for d in range(1, sources)]
    held = held + [swap(block, "dp", 2) for block in held]
    held = held + [swap(block, "dp", 1) for block in held]

    gate_value = jax.nn.sigmoid(
        jnp.dot(norm_input, shared_gate, preferred_element_type=F32)
    )
    inner = jnp.sum(out_grad.astype(F32) * shared_out.astype(F32), axis=1)
    gate_delta = inner * gate_value * (1.0 - gate_value)
    gate_local = jnp.sum(gate_delta[:, None] * norm_input.astype(F32), axis=0)
    share = features // tokens
    tail = jnp.pad(gate_local.reshape(tokens, share), ((0, 0), (TOPK, LANES - TOPK - share)))

    kept, sent = run_experts(held, tail, w_gate, w_up, w_down, sources)
    total = (kept.astype(F32) + swap(sent, "dp", 1).astype(F32)).astype(BF16)
    half = total.shape[0] // 2
    total = (total[:half].astype(F32) + swap(total[half:], "dp", 2).astype(F32)).astype(BF16)
    final = total[:tokens].astype(F32)
    for d in range(1, sources):
        final = final + swap(total[d * tokens : (d + 1) * tokens], "expert", d).astype(F32)
    input_grad = (
        final[:, :features] + gate_delta[:, None] * shared_gate.astype(F32)[None, :]
    ).astype(BF16)
    route_grad = final[:, features : features + TOPK]
    gate_grad = final[:, features + TOPK : features + TOPK + share].reshape(features)
    return (input_grad, route_grad, gate_grad)


def solution(mesh):
    square = mesh.shape["expert"] == 4 and mesh.shape["dp"] == 4
    on_device = square_device if square else general_device
    return jax.shard_map(
        on_device,
        mesh=mesh,
        in_specs=(
            P(("groups", "expert", "dp"), None),
            P(("groups", "expert", "dp"), None),
            P(("groups", "expert", "dp"), None),
            P(("groups", "expert", "dp"), None),
            P(("groups", "expert", "dp"), None),
            P(),
            P("expert", None, "dp"),
            P("expert", None, "dp"),
            P("expert", "dp", None),
        ),
        out_specs=(
            P(("groups", "expert", "dp"), None),
            P(("groups", "expert", "dp"), None),
            P("groups"),
        ),
        check_vma=False,
    )
```

```python
import functools

import jax
import jax.numpy as jnp
import numpy as np
from jax import lax
from jax.experimental import pallas as pl
from jax.experimental.pallas import tpu as pltpu
from jax.sharding import PartitionSpec as P

EXPERTS = 64
TOPK = 8
CAP = 12
LANES = 128
BF16 = jnp.bfloat16
F32 = jnp.float32
NT = (((1,), (1,)), ((), ()))
TN = (((0,), (0,)), ((), ()))


def slot_targets(group_ids):
    flat_ids = group_ids.reshape(-1)
    one_hot = (flat_ids[:, None] == jnp.arange(EXPERTS, dtype=jnp.int32)[None, :]).astype(jnp.int32)
    before = jnp.cumsum(one_hot, axis=0) - one_hot
    position = jnp.sum(before * one_hot, axis=1)
    return flat_ids * CAP + position


def general_device(
    norm_input, out_grad, shared_out, expert_ids, route_weight, shared_gate, w_gate, w_up, w_down
):
    features = norm_input.shape[1]
    group_norm, group_grad, group_codes, group_weight = (
        lax.all_gather(norm_input, "dp", axis=0, tiled=True),
        lax.all_gather(out_grad, "dp", axis=0, tiled=True),
        lax.all_gather(expert_ids.astype(jnp.bfloat16), "dp", axis=0, tiled=True),
        lax.all_gather(route_weight, "dp", axis=0, tiled=True),
    )
    group_ids = group_codes.astype(jnp.int32)
    group_tokens = group_norm.shape[0]
    target = slot_targets(group_ids)
    slots = jnp.arange(EXPERTS * CAP, dtype=jnp.int32)
    hits = (target[None, :] == slots[:, None]).astype(jnp.bfloat16)
    dispatch = hits.reshape(EXPERTS * CAP, group_tokens, TOPK).sum(axis=2)
    slot_norm = jnp.dot(dispatch, group_norm, preferred_element_type=jnp.float32).astype(
        jnp.bfloat16
    )
    slot_grad = jnp.dot(dispatch, group_grad, preferred_element_type=jnp.float32).astype(
        jnp.bfloat16
    )
    slot_norm = slot_norm.reshape(EXPERTS, CAP, features)
    slot_grad = slot_grad.reshape(EXPERTS, CAP, features)
    local_experts = w_gate.shape[0]
    quarter = CAP // lax.axis_size("dp")
    offset = lax.axis_index("dp") * quarter
    norm_share = lax.dynamic_slice_in_dim(slot_norm, offset, quarter, 1)
    grad_share = lax.dynamic_slice_in_dim(slot_grad, offset, quarter, 1)
    arrived_norm, arrived_grad = (
        lax.all_to_all(norm_share, "expert", split_axis=0, concat_axis=0, tiled=True),
        lax.all_to_all(grad_share, "expert", split_axis=0, concat_axis=0, tiled=True),
    )
    rows_in = lax.all_gather(arrived_norm, "dp", axis=1, tiled=True)
    grads_in = lax.all_gather(arrived_grad, "dp", axis=1, tiled=True)
    item_count = rows_in.shape[1]
    sources = rows_in.shape[0] // local_experts
    rows_four = rows_in.reshape(sources, local_experts, item_count, features)
    grads_four = grads_in.reshape(sources, local_experts, item_count, features)
    gate_pre = jnp.einsum("sxcd,xdf->sxcf", rows_four, w_gate, preferred_element_type=jnp.float32)
    up_pre = jnp.einsum("sxcd,xdf->sxcf", rows_four, w_up, preferred_element_type=jnp.float32)
    hidden_grad = jnp.einsum(
        "sxcd,xfd->sxcf", grads_four, w_down, preferred_element_type=jnp.float32
    )
    logistic = jax.nn.sigmoid(gate_pre)
    swish = gate_pre * logistic
    act = swish * up_pre
    gate_diff = (hidden_grad * up_pre * logistic * (1.0 + gate_pre * (1.0 - logistic))).astype(
        jnp.bfloat16
    )
    up_diff = (hidden_grad * swish).astype(jnp.bfloat16)
    row_part = jnp.einsum("sxcf,xdf->sxcd", gate_diff, w_gate, preferred_element_type=jnp.float32)
    row_part = row_part + jnp.einsum(
        "sxcf,xdf->sxcd", up_diff, w_up, preferred_element_type=jnp.float32
    )
    row_back = row_part.astype(jnp.bfloat16).reshape(sources * local_experts, item_count, features)
    score_back = jnp.sum(act * hidden_grad, axis=3).astype(jnp.bfloat16)
    score_back = score_back.reshape(sources * local_experts, item_count, 1)
    back_rows = lax.all_to_all(row_back, "expert", split_axis=0, concat_axis=0, tiled=True)
    back_scores = lax.all_to_all(score_back, "expert", split_axis=0, concat_axis=0, tiled=True)
    columns = back_rows.shape[2]
    back_flat = back_rows.reshape(EXPERTS * CAP, columns)
    score_flat = back_scores.reshape(EXPERTS * CAP)
    picked = jnp.take(back_flat, target, axis=0).reshape(group_tokens, TOPK, columns)
    token_part = jnp.einsum(
        "tk,tkd->td", group_weight.astype(jnp.float32), picked.astype(jnp.float32)
    )
    score_part = (
        jnp.take(score_flat, target, axis=0).astype(jnp.float32).reshape(group_tokens, TOPK)
    )
    routed, route_grad = (
        lax.psum_scatter(
            token_part.astype(jnp.bfloat16), "dp", scatter_dimension=0, tiled=True
        ).astype(jnp.float32),
        lax.psum_scatter(
            score_part.astype(jnp.bfloat16), "dp", scatter_dimension=0, tiled=True
        ).astype(jnp.float32),
    )
    gate_value = jax.nn.sigmoid(
        jnp.dot(norm_input, shared_gate, preferred_element_type=jnp.float32)
    )
    inner = jnp.sum(out_grad.astype(jnp.float32) * shared_out.astype(jnp.float32), axis=1)
    gate_delta = inner * gate_value * (1.0 - gate_value)
    input_grad = (routed + gate_delta[:, None] * shared_gate.astype(jnp.float32)[None, :]).astype(
        jnp.bfloat16
    )
    gate_local = jnp.dot(
        gate_delta, norm_input.astype(jnp.float32), precision=lax.Precision.HIGHEST
    )
    gate_grad = lax.psum(gate_local, ("expert", "dp"))
    return (input_grad, route_grad, gate_grad)


def dot(a, b, dims=(((1,), (0,)), ((), ()))):
    return lax.dot_general(a, b, dims, preferred_element_type=F32)


def swap(value, axis, distance):
    size = lax.axis_size(axis)
    return lax.ppermute(value, axis, [(i, i ^ distance) for i in range(size)])


def experts_kernel(features, rows, blocks, group, *refs):
    token_refs, refs = refs[:blocks], refs[blocks:]
    tail_ref, w_gate, w_up, w_down, keep_ref, send_ref, tokens, copied, gates, ups, downs, loaded, spread, weighted, norms, grads, backs, hits, routes = refs
    number = w_gate.shape[0]
    starts = np.cumsum([0] + [ref.shape[0] for ref in token_refs])
    count = int(starts[-1])

    def loads(turn, k):
        expert = turn * group + k
        slot = lax.rem(turn, 3) * group + k
        return [
            pltpu.make_async_copy(source.at[expert], target.at[slot], loaded.at[slot, j])
            for j, (source, target) in enumerate(((w_gate, gates), (w_up, ups), (w_down, downs)))
        ]

    copies = [
        pltpu.make_async_copy(ref, tokens.at[pl.ds(int(starts[j]), ref.shape[0])], copied.at[j])
        for j, ref in enumerate(token_refs)
    ]
    for copy in copies:
        copy.start()
    for copy in copies:
        copy.wait()
    for k in range(group):
        for copy in loads(0, k):
            copy.start()
    for k in range(group):
        for copy in loads(1, k):
            copy.start()
    codes = tokens[:, 2 * features :].astype(F32).T
    weights = codes[TOPK : 2 * TOPK]
    local = codes[:TOPK] - (lax.axis_index("expert") * number).astype(F32)
    hits[...] = local
    earlier = (
        lax.broadcasted_iota(jnp.int32, (count, count), 0)
        < lax.broadcasted_iota(jnp.int32, (count, count), 1)
    ).astype(BF16)
    masks = [local == float(e) for e in range(number)]
    member = jnp.concatenate(
        [jnp.sum(m.astype(F32), axis=0, keepdims=True) for m in masks], axis=0
    )
    position = dot(member.astype(BF16), earlier)
    slot = lax.broadcasted_iota(jnp.int32, (rows, count), 0).astype(F32)
    for e in range(number):
        weight = jnp.sum(jnp.where(masks[e], weights, 0.0), axis=0, keepdims=True)
        chosen = (slot == position[e : e + 1]) & (member[e : e + 1] > 0.0)
        spread[e * rows : (e + 1) * rows] = jnp.where(chosen, 1.0, 0.0).astype(BF16)
        weighted[e * rows : (e + 1) * rows] = jnp.where(chosen, weight, 0.0).astype(BF16)
    norms[...] = dot(spread[...], tokens[:, :features]).astype(BF16)
    grads[...] = dot(spread[...], tokens[:, features : 2 * features]).astype(BF16)
    routes[...] = jnp.zeros_like(routes)

    def run(turn, _):
        base = lax.rem(turn, 3) * group
        heres = [
            pl.ds(pl.multiple_of((turn * group + k) * rows, rows), rows) for k in range(group)
        ]
        for k in range(group):
            for copy in loads(turn, k):
                copy.wait()
        @pl.when(turn + 2 < number // group)
        def _():
            for k in range(group):
                for copy in loads(turn + 2, k):
                    copy.start()

        pre = []
        for k in range(group):
            x, dy = norms[heres[k]], grads[heres[k]]
            pre.append((dot(x, gates[base + k]), dot(x, ups[base + k]), dot(dy, downs[base + k], NT)))
        for k in range(group):
            gate_pre, up_pre, hidden_grad = pre[k]
            logistic = jax.nn.sigmoid(gate_pre)
            swish = gate_pre * logistic
            gate_diff = (
                hidden_grad * up_pre * logistic * (1.0 + gate_pre * (1.0 - logistic))
            ).astype(BF16)
            up_diff = (hidden_grad * swish).astype(BF16)
            first_part = dot(gate_diff, gates[base + k], NT)
            second_part = dot(ups[base + k], up_diff, NT).T
            backs[heres[k]] = (first_part + second_part).astype(BF16)
            score = jnp.sum(swish * up_pre * hidden_grad, axis=1, keepdims=True)
            by_token = jnp.sum(spread[heres[k]].astype(F32) * score, axis=0, keepdims=True)
            here = (turn * group + k).astype(F32)
            routes[...] += jnp.where(hits[...] == here, by_token, 0.0)

        return 0

    lax.fori_loop(0, number // group, run, 0)
    half = count // 2
    result = dot(weighted[...], backs[...], TN).astype(BF16)
    each = tail_ref.shape[0]
    line = features // LANES
    token = lax.broadcasted_iota(jnp.int32, (count, LANES), 0)
    lane = lax.broadcasted_iota(jnp.int32, (count, LANES), 1)
    repeat = (
        lax.broadcasted_iota(jnp.int32, (TOPK, LANES), 1) % TOPK
        == lax.broadcasted_iota(jnp.int32, (TOPK, LANES), 0)
    ).astype(BF16)
    scores = dot(routes[...].astype(BF16), repeat, TN)
    scores = jnp.where(lane // TOPK == token % each, scores, 0.0).astype(BF16)
    row = lax.broadcasted_iota(jnp.int32, (count, count), 0)
    column = lax.broadcasted_iota(jnp.int32, (count, count), 1)
    gather = ((row % each == line) & (row // each == column // each)).astype(BF16)
    tail = jnp.concatenate([tail_ref[...]] * (count // each), axis=0)
    last = (dot(gather, scores) + tail).astype(BF16)
    keep_ref[:, :features] = result[:half]
    send_ref[:, :features] = result[half:]
    keep_ref[:, features:] = last[:half]
    send_ref[:, features:] = last[half:]


def run_experts(token_blocks, tail, w_gate, w_up, w_down, sources):
    local, features, hidden = w_gate.shape
    blocks = len(token_blocks)
    count = sum(block.shape[0] for block in token_blocks)
    rows = sources * CAP
    width = features + LANES
    group = 2
    away = pl.BlockSpec(memory_space=pl.ANY)
    near = pl.BlockSpec(memory_space=pltpu.VMEM)
    return pl.pallas_call(
        functools.partial(experts_kernel, features, rows, blocks, group),
        in_specs=[away] * blocks + [near, away, away, away],
        out_specs=[near] * 2,
        out_shape=[jax.ShapeDtypeStruct((count // 2, width), BF16)] * 2,
        scratch_shapes=[
            pltpu.VMEM((count, 2 * features + LANES), BF16),
            pltpu.SemaphoreType.DMA((blocks,)),
            pltpu.VMEM((3 * group, features, hidden), BF16),
            pltpu.VMEM((3 * group, features, hidden), BF16),
            pltpu.VMEM((3 * group, hidden, features), BF16),
            pltpu.SemaphoreType.DMA((3 * group, 3)),
            pltpu.VMEM((local * rows, count), BF16),
            pltpu.VMEM((local * rows, count), BF16),
            pltpu.VMEM((local * rows, features), BF16),
            pltpu.VMEM((local * rows, features), BF16),
            pltpu.VMEM((local * rows, features), BF16),
            pltpu.VMEM((TOPK, count), F32),
            pltpu.VMEM((TOPK, count), F32),
        ],
        compiler_params=pltpu.CompilerParams(vmem_limit_bytes=44 << 20),
        name="experts",
    )(*token_blocks, tail, w_gate, w_up, w_down)


def pack_kernel(norm_ref, grad_ref, shared_ref, ids_ref, weight_ref, gate_ref, packed_ref, tail_ref, term_ref):
    tokens, features = norm_ref.shape
    norm = norm_ref[...].astype(F32)
    grad = grad_ref[...].astype(F32)
    gate = gate_ref[...].astype(F32)
    packed_ref[:, :features] = norm_ref[...]
    packed_ref[:, features : 2 * features] = grad_ref[...]
    lane = lax.broadcasted_iota(jnp.int32, (TOPK, LANES), 1)
    source = lax.broadcasted_iota(jnp.int32, (TOPK, LANES), 0)
    ids = ids_ref[...].astype(F32).astype(BF16)
    codes = dot(ids, (lane == source).astype(BF16)) + dot(
        weight_ref[...], (lane == source + TOPK).astype(BF16)
    )
    packed_ref[:, 2 * features :] = codes.astype(BF16)
    gate_value = jax.nn.sigmoid(jnp.sum(norm * gate, axis=1, keepdims=True))
    inner = jnp.sum(grad * shared_ref[...].astype(F32), axis=1, keepdims=True)
    delta = inner * gate_value * (1.0 - gate_value)
    term_ref[...] = delta * gate
    local = jnp.sum(delta * norm, axis=0, keepdims=True)
    tail_ref[...] = jnp.zeros_like(tail_ref)
    for r in range(features // LANES):
        tail_ref[r : r + 1, :] = local[:, r * LANES : (r + 1) * LANES]


def pack(norm_input, out_grad, shared_out, expert_ids, route_weight, shared_gate):
    tokens, features = norm_input.shape
    return pl.pallas_call(
        pack_kernel,
        out_shape=[
            jax.ShapeDtypeStruct((tokens, 2 * features + LANES), BF16),
            jax.ShapeDtypeStruct((tokens, LANES), F32),
            jax.ShapeDtypeStruct((tokens, features), F32),
        ],
        compiler_params=pltpu.CompilerParams(vmem_limit_bytes=4 << 20),
        name="pack",
    )(norm_input, out_grad, shared_out, expert_ids, route_weight, shared_gate[None, :])


def finish_kernel(total_ref, *refs):
    parts, (term_ref, input_ref, route_ref, gate_ref) = refs[:-4], refs[-4:]
    tokens, features = term_ref.shape
    final = total_ref[:tokens].astype(F32)
    for part in parts:
        final = final + part[...].astype(F32)
    input_ref[...] = (final[:, :features] + term_ref[...]).astype(BF16)
    line = features // LANES
    gate_ref[...] = final[:line, features:]
    lane = lax.broadcasted_iota(jnp.int32, (tokens, LANES), 1)
    token = lax.broadcasted_iota(jnp.int32, (tokens, LANES), 0)
    spread = jnp.where(lane // TOPK == token, final[line : line + 1, features:], 0.0)
    choose = (
        lax.broadcasted_iota(jnp.int32, (LANES, TOPK), 0) % TOPK
        == lax.broadcasted_iota(jnp.int32, (LANES, TOPK), 1)
    ).astype(F32)
    route_ref[...] = jnp.dot(
        spread, choose, precision=lax.Precision.HIGHEST, preferred_element_type=F32
    )


def finish(total, parts, term):
    tokens, features = term.shape
    return pl.pallas_call(
        finish_kernel,
        out_shape=[
            jax.ShapeDtypeStruct((tokens, features), BF16),
            jax.ShapeDtypeStruct((tokens, TOPK), F32),
            jax.ShapeDtypeStruct((features // LANES, LANES), F32),
        ],
        compiler_params=pltpu.CompilerParams(vmem_limit_bytes=4 << 20),
        name="finish",
    )(total, *parts, term)


def square_device(
    norm_input, out_grad, shared_out, expert_ids, route_weight, shared_gate, w_gate, w_up, w_down
):
    tokens, features = norm_input.shape
    sources = lax.axis_size("expert")
    mine, tail, term = pack(
        norm_input, out_grad, shared_out, expert_ids, route_weight, shared_gate
    )
    along = [mine] + [swap(mine, "expert", d) for d in range(1, sources)]
    near, far = jnp.concatenate(along[:2], axis=0), jnp.concatenate(along[2:], axis=0)
    near_x, far_x = swap(near, "dp", 2), swap(far, "dp", 2)
    both = jnp.concatenate([near, far], axis=0)
    held = [near, far, near_x, far_x]
    held += [swap(block, "dp", 1) for block in (both, near_x, far_x)]
    kept, sent = run_experts(held, tail, w_gate, w_up, w_down, sources)
    total = (kept.astype(F32) + swap(sent, "dp", 1).astype(F32)).astype(BF16)
    half = total.shape[0] // 2
    total = (total[:half].astype(F32) + swap(total[half:], "dp", 2).astype(F32)).astype(BF16)
    parts = [
        swap(total[d * tokens : (d + 1) * tokens], "expert", d) for d in range(sources - 1, 0, -1)
    ]
    input_grad, route_grad, gate_grad = finish(total, parts, term)
    return (input_grad, route_grad, gate_grad.reshape(features))


def solution(mesh):
    square = mesh.shape["expert"] == 4 and mesh.shape["dp"] == 4
    on_device = square_device if square else general_device
    return jax.shard_map(
        on_device,
        mesh=mesh,
        in_specs=(
            P(("groups", "expert", "dp"), None),
            P(("groups", "expert", "dp"), None),
            P(("groups", "expert", "dp"), None),
            P(("groups", "expert", "dp"), None),
            P(("groups", "expert", "dp"), None),
            P(),
            P("expert", None, "dp"),
            P("expert", None, "dp"),
            P("expert", "dp", None),
        ),
        out_specs=(
            P(("groups", "expert", "dp"), None),
            P(("groups", "expert", "dp"), None),
            P("groups"),
        ),
        check_vma=False,
    )
```

```python
import functools

import jax
import jax.numpy as jnp
import numpy as np
from jax import lax
from jax.experimental import pallas as pl
from jax.experimental.pallas import tpu as pltpu
from jax.sharding import PartitionSpec as P

EXPERTS = 64
TOPK = 8
CAP = 12
LANES = 128
BF16 = jnp.bfloat16
F32 = jnp.float32
NT = (((1,), (1,)), ((), ()))
TN = (((0,), (0,)), ((), ()))


def slot_targets(group_ids):
    flat_ids = group_ids.reshape(-1)
    one_hot = (flat_ids[:, None] == jnp.arange(EXPERTS, dtype=jnp.int32)[None, :]).astype(jnp.int32)
    before = jnp.cumsum(one_hot, axis=0) - one_hot
    position = jnp.sum(before * one_hot, axis=1)
    return flat_ids * CAP + position


def general_device(
    norm_input, out_grad, shared_out, expert_ids, route_weight, shared_gate, w_gate, w_up, w_down
):
    features = norm_input.shape[1]
    group_norm, group_grad, group_codes, group_weight = (
        lax.all_gather(norm_input, "dp", axis=0, tiled=True),
        lax.all_gather(out_grad, "dp", axis=0, tiled=True),
        lax.all_gather(expert_ids.astype(jnp.bfloat16), "dp", axis=0, tiled=True),
        lax.all_gather(route_weight, "dp", axis=0, tiled=True),
    )
    group_ids = group_codes.astype(jnp.int32)
    group_tokens = group_norm.shape[0]
    target = slot_targets(group_ids)
    slots = jnp.arange(EXPERTS * CAP, dtype=jnp.int32)
    hits = (target[None, :] == slots[:, None]).astype(jnp.bfloat16)
    dispatch = hits.reshape(EXPERTS * CAP, group_tokens, TOPK).sum(axis=2)
    slot_norm = jnp.dot(dispatch, group_norm, preferred_element_type=jnp.float32).astype(
        jnp.bfloat16
    )
    slot_grad = jnp.dot(dispatch, group_grad, preferred_element_type=jnp.float32).astype(
        jnp.bfloat16
    )
    slot_norm = slot_norm.reshape(EXPERTS, CAP, features)
    slot_grad = slot_grad.reshape(EXPERTS, CAP, features)
    local_experts = w_gate.shape[0]
    quarter = CAP // lax.axis_size("dp")
    offset = lax.axis_index("dp") * quarter
    norm_share = lax.dynamic_slice_in_dim(slot_norm, offset, quarter, 1)
    grad_share = lax.dynamic_slice_in_dim(slot_grad, offset, quarter, 1)
    arrived_norm, arrived_grad = (
        lax.all_to_all(norm_share, "expert", split_axis=0, concat_axis=0, tiled=True),
        lax.all_to_all(grad_share, "expert", split_axis=0, concat_axis=0, tiled=True),
    )
    rows_in = lax.all_gather(arrived_norm, "dp", axis=1, tiled=True)
    grads_in = lax.all_gather(arrived_grad, "dp", axis=1, tiled=True)
    item_count = rows_in.shape[1]
    sources = rows_in.shape[0] // local_experts
    rows_four = rows_in.reshape(sources, local_experts, item_count, features)
    grads_four = grads_in.reshape(sources, local_experts, item_count, features)
    gate_pre = jnp.einsum("sxcd,xdf->sxcf", rows_four, w_gate, preferred_element_type=jnp.float32)
    up_pre = jnp.einsum("sxcd,xdf->sxcf", rows_four, w_up, preferred_element_type=jnp.float32)
    hidden_grad = jnp.einsum(
        "sxcd,xfd->sxcf", grads_four, w_down, preferred_element_type=jnp.float32
    )
    logistic = jax.nn.sigmoid(gate_pre)
    swish = gate_pre * logistic
    act = swish * up_pre
    gate_diff = (hidden_grad * up_pre * logistic * (1.0 + gate_pre * (1.0 - logistic))).astype(
        jnp.bfloat16
    )
    up_diff = (hidden_grad * swish).astype(jnp.bfloat16)
    row_part = jnp.einsum("sxcf,xdf->sxcd", gate_diff, w_gate, preferred_element_type=jnp.float32)
    row_part = row_part + jnp.einsum(
        "sxcf,xdf->sxcd", up_diff, w_up, preferred_element_type=jnp.float32
    )
    row_back = row_part.astype(jnp.bfloat16).reshape(sources * local_experts, item_count, features)
    score_back = jnp.sum(act * hidden_grad, axis=3).astype(jnp.bfloat16)
    score_back = score_back.reshape(sources * local_experts, item_count, 1)
    back_rows = lax.all_to_all(row_back, "expert", split_axis=0, concat_axis=0, tiled=True)
    back_scores = lax.all_to_all(score_back, "expert", split_axis=0, concat_axis=0, tiled=True)
    columns = back_rows.shape[2]
    back_flat = back_rows.reshape(EXPERTS * CAP, columns)
    score_flat = back_scores.reshape(EXPERTS * CAP)
    picked = jnp.take(back_flat, target, axis=0).reshape(group_tokens, TOPK, columns)
    token_part = jnp.einsum(
        "tk,tkd->td", group_weight.astype(jnp.float32), picked.astype(jnp.float32)
    )
    score_part = (
        jnp.take(score_flat, target, axis=0).astype(jnp.float32).reshape(group_tokens, TOPK)
    )
    routed, route_grad = (
        lax.psum_scatter(
            token_part.astype(jnp.bfloat16), "dp", scatter_dimension=0, tiled=True
        ).astype(jnp.float32),
        lax.psum_scatter(
            score_part.astype(jnp.bfloat16), "dp", scatter_dimension=0, tiled=True
        ).astype(jnp.float32),
    )
    gate_value = jax.nn.sigmoid(
        jnp.dot(norm_input, shared_gate, preferred_element_type=jnp.float32)
    )
    inner = jnp.sum(out_grad.astype(jnp.float32) * shared_out.astype(jnp.float32), axis=1)
    gate_delta = inner * gate_value * (1.0 - gate_value)
    input_grad = (routed + gate_delta[:, None] * shared_gate.astype(jnp.float32)[None, :]).astype(
        jnp.bfloat16
    )
    gate_local = jnp.dot(
        gate_delta, norm_input.astype(jnp.float32), precision=lax.Precision.HIGHEST
    )
    gate_grad = lax.psum(gate_local, ("expert", "dp"))
    return (input_grad, route_grad, gate_grad)


def dot(a, b, dims=(((1,), (0,)), ((), ()))):
    return lax.dot_general(a, b, dims, preferred_element_type=F32)


def swap(value, axis, distance):
    size = lax.axis_size(axis)
    return lax.ppermute(value, axis, [(i, i ^ distance) for i in range(size)])


def experts_kernel(features, rows, blocks, group, *refs):
    token_refs, refs = refs[:blocks], refs[blocks:]
    tail_ref, w_gate, w_up, w_down, keep_ref, send_ref, tokens, copied, gates, ups, downs, loaded, spread, weighted, norms, grads, backs, hits, routes = refs
    number = w_gate.shape[0]
    starts = np.cumsum([0] + [ref.shape[0] for ref in token_refs])
    count = int(starts[-1])

    def loads(turn, k):
        expert = turn * group + k
        slot = lax.rem(turn, 3) * group + k
        return [
            pltpu.make_async_copy(source.at[expert], target.at[slot], loaded.at[slot, j])
            for j, (source, target) in enumerate(((w_gate, gates), (w_up, ups), (w_down, downs)))
        ]

    copies = [
        pltpu.make_async_copy(ref, tokens.at[pl.ds(int(starts[j]), ref.shape[0])], copied.at[j])
        for j, ref in enumerate(token_refs)
    ]
    for copy in copies:
        copy.start()
    for copy in copies:
        copy.wait()
    for k in range(group):
        for copy in loads(0, k):
            copy.start()
    for k in range(group):
        for copy in loads(1, k):
            copy.start()
    codes = tokens[:, 2 * features :].astype(F32).T
    weights = codes[TOPK : 2 * TOPK]
    local = codes[:TOPK] - (lax.axis_index("expert") * number).astype(F32)
    hits[...] = local
    earlier = (
        lax.broadcasted_iota(jnp.int32, (count, count), 0)
        < lax.broadcasted_iota(jnp.int32, (count, count), 1)
    ).astype(BF16)
    masks = [local == float(e) for e in range(number)]
    member = jnp.concatenate(
        [jnp.sum(m.astype(F32), axis=0, keepdims=True) for m in masks], axis=0
    )
    position = dot(member.astype(BF16), earlier)
    slot = lax.broadcasted_iota(jnp.int32, (rows, count), 0).astype(F32)
    for e in range(number):
        weight = jnp.sum(jnp.where(masks[e], weights, 0.0), axis=0, keepdims=True)
        chosen = (slot == position[e : e + 1]) & (member[e : e + 1] > 0.0)
        spread[e * rows : (e + 1) * rows] = jnp.where(chosen, 1.0, 0.0).astype(BF16)
        weighted[e * rows : (e + 1) * rows] = jnp.where(chosen, weight, 0.0).astype(BF16)
    norms[...] = dot(spread[...], tokens[:, :features]).astype(BF16)
    grads[...] = dot(spread[...], tokens[:, features : 2 * features]).astype(BF16)
    routes[...] = jnp.zeros_like(routes)

    def run(turn, _):
        base = lax.rem(turn, 3) * group
        heres = [
            pl.ds(pl.multiple_of((turn * group + k) * rows, rows), rows) for k in range(group)
        ]
        for k in range(group):
            for copy in loads(turn, k):
                copy.wait()
        @pl.when(turn + 2 < number // group)
        def _():
            for k in range(group):
                for copy in loads(turn + 2, k):
                    copy.start()

        pre = []
        for k in range(group):
            x, dy = norms[heres[k]], grads[heres[k]]
            pre.append((dot(x, gates[base + k]), dot(x, ups[base + k]), dot(dy, downs[base + k], NT)))
        for k in range(group):
            gate_pre, up_pre, hidden_grad = pre[k]
            logistic = jax.nn.sigmoid(gate_pre)
            swish = gate_pre * logistic
            gate_diff = (
                hidden_grad * up_pre * logistic * (1.0 + gate_pre * (1.0 - logistic))
            ).astype(BF16)
            up_diff = (hidden_grad * swish).astype(BF16)
            first_part = dot(gate_diff, gates[base + k], NT)
            second_part = dot(ups[base + k], up_diff, NT).T
            backs[heres[k]] = (first_part + second_part).astype(BF16)
            score = jnp.sum(swish * up_pre * hidden_grad, axis=1, keepdims=True)
            by_token = jnp.sum(spread[heres[k]].astype(F32) * score, axis=0, keepdims=True)
            here = (turn * group + k).astype(F32)
            routes[...] += jnp.where(hits[...] == here, by_token, 0.0)

        return 0

    lax.fori_loop(0, number // group, run, 0)
    half = count // 2
    result = dot(weighted[...], backs[...], TN).astype(BF16)
    each = tail_ref.shape[0]
    line = features // LANES
    token = lax.broadcasted_iota(jnp.int32, (count, LANES), 0)
    lane = lax.broadcasted_iota(jnp.int32, (count, LANES), 1)
    repeat = (
        lax.broadcasted_iota(jnp.int32, (TOPK, LANES), 1) % TOPK
        == lax.broadcasted_iota(jnp.int32, (TOPK, LANES), 0)
    ).astype(BF16)
    scores = dot(routes[...].astype(BF16), repeat, TN)
    scores = jnp.where(lane // TOPK == token % each, scores, 0.0).astype(BF16)
    row = lax.broadcasted_iota(jnp.int32, (count, count), 0)
    column = lax.broadcasted_iota(jnp.int32, (count, count), 1)
    gather = ((row % each == line) & (row // each == column // each)).astype(BF16)
    tail = jnp.concatenate([tail_ref[...]] * (count // each), axis=0)
    last = (dot(gather, scores) + tail).astype(BF16)
    keep_ref[:, :features] = result[:half]
    send_ref[:, :features] = result[half:]
    keep_ref[:, features:] = last[:half]
    send_ref[:, features:] = last[half:]


def run_experts(token_blocks, tail, w_gate, w_up, w_down, sources):
    local, features, hidden = w_gate.shape
    blocks = len(token_blocks)
    count = sum(block.shape[0] for block in token_blocks)
    rows = sources * CAP
    width = features + LANES
    group = 2
    away = pl.BlockSpec(memory_space=pl.ANY)
    near = pl.BlockSpec(memory_space=pltpu.VMEM)
    return pl.pallas_call(
        functools.partial(experts_kernel, features, rows, blocks, group),
        in_specs=[away] * blocks + [near, away, away, away],
        out_specs=[near] * 2,
        out_shape=[jax.ShapeDtypeStruct((count // 2, width), BF16)] * 2,
        scratch_shapes=[
            pltpu.VMEM((count, 2 * features + LANES), BF16),
            pltpu.SemaphoreType.DMA((blocks,)),
            pltpu.VMEM((3 * group, features, hidden), BF16),
            pltpu.VMEM((3 * group, features, hidden), BF16),
            pltpu.VMEM((3 * group, hidden, features), BF16),
            pltpu.SemaphoreType.DMA((3 * group, 3)),
            pltpu.VMEM((local * rows, count), BF16),
            pltpu.VMEM((local * rows, count), BF16),
            pltpu.VMEM((local * rows, features), BF16),
            pltpu.VMEM((local * rows, features), BF16),
            pltpu.VMEM((local * rows, features), BF16),
            pltpu.VMEM((TOPK, count), F32),
            pltpu.VMEM((TOPK, count), F32),
        ],
        compiler_params=pltpu.CompilerParams(vmem_limit_bytes=44 << 20),
        name="experts",
    )(*token_blocks, tail, w_gate, w_up, w_down)


def in_hbm(value):
    return pltpu.with_memory_space_constraint(value, pltpu.HBM)


def pack_kernel(norm_ref, grad_ref, ids_ref, weight_ref, packed_ref, copied):
    features = norm_ref.shape[1]
    copies = [
        pltpu.make_async_copy(ref, packed_ref.at[:, pl.ds(j * features, features)], copied.at[j])
        for j, ref in enumerate((norm_ref, grad_ref))
    ]
    for copy in copies:
        copy.start()
    lane = lax.broadcasted_iota(jnp.int32, (TOPK, LANES), 1)
    source = lax.broadcasted_iota(jnp.int32, (TOPK, LANES), 0)
    ids = ids_ref[...].astype(F32).astype(BF16)
    codes = dot(ids, (lane == source).astype(BF16), TN) + dot(
        weight_ref[...], (lane == source + TOPK).astype(BF16), TN
    )
    packed_ref[:, 2 * features :] = codes.astype(BF16)
    for copy in copies:
        copy.wait()


def pack(norm_input, out_grad, expert_ids, route_weight):
    tokens, features = norm_input.shape
    away = pl.BlockSpec(memory_space=pltpu.HBM)
    near = pl.BlockSpec(memory_space=pltpu.VMEM)
    return pl.pallas_call(
        pack_kernel,
        in_specs=[away, away, near, near],
        out_specs=near,
        out_shape=jax.ShapeDtypeStruct((tokens, 2 * features + LANES), BF16),
        scratch_shapes=[pltpu.SemaphoreType.DMA((2,))],
        compiler_params=pltpu.CompilerParams(vmem_limit_bytes=4 << 20),
        name="pack",
    )(*map(in_hbm, (norm_input, out_grad, expert_ids.T, route_weight.T)))


def shared_kernel(norm_ref, grad_ref, shared_ref, gate_ref, tail_ref, term_ref, copied, norms, grads, outs):
    features = norm_ref.shape[1]
    copies = [
        pltpu.make_async_copy(ref, target, copied.at[j])
        for j, (ref, target) in enumerate(((norm_ref, norms), (grad_ref, grads), (shared_ref, outs)))
    ]
    for copy in copies:
        copy.start()
    for copy in copies:
        copy.wait()
    norm = norms[...].astype(F32)
    gate = gate_ref[...].astype(F32)
    gate_value = jax.nn.sigmoid(jnp.sum(norm * gate, axis=1, keepdims=True))
    inner = jnp.sum(grads[...].astype(F32) * outs[...].astype(F32), axis=1, keepdims=True)
    delta = inner * gate_value * (1.0 - gate_value)
    term_ref[...] = delta * gate
    local = jnp.sum(delta * norm, axis=0, keepdims=True)
    tail_ref[...] = jnp.zeros_like(tail_ref)
    for r in range(features // LANES):
        tail_ref[r : r + 1, :] = local[:, r * LANES : (r + 1) * LANES]


def shared(norm_input, out_grad, shared_out, shared_gate):
    tokens, features = norm_input.shape
    away = pl.BlockSpec(memory_space=pltpu.HBM)
    near = pl.BlockSpec(memory_space=pltpu.VMEM)
    return pl.pallas_call(
        shared_kernel,
        in_specs=[away, away, away, near],
        out_specs=[near, near],
        out_shape=[
            jax.ShapeDtypeStruct((tokens, LANES), F32),
            jax.ShapeDtypeStruct((tokens, features), F32),
        ],
        scratch_shapes=[pltpu.SemaphoreType.DMA((3,))]
        + [pltpu.VMEM((tokens, features), BF16)] * 3,
        compiler_params=pltpu.CompilerParams(vmem_limit_bytes=4 << 20),
        name="shared",
    )(*map(in_hbm, (norm_input, out_grad, shared_out)), shared_gate[None, :])


def finish_kernel(total_ref, *refs):
    parts, (term_ref, input_ref, route_ref, gate_ref) = refs[:-4], refs[-4:]
    tokens, features = term_ref.shape
    final = total_ref[:tokens].astype(F32)
    for part in parts:
        final = final + part[...].astype(F32)
    input_ref[...] = (final[:, :features] + term_ref[...]).astype(BF16)
    line = features // LANES
    gate_ref[...] = final[:line, features:]
    lane = lax.broadcasted_iota(jnp.int32, (tokens, LANES), 1)
    token = lax.broadcasted_iota(jnp.int32, (tokens, LANES), 0)
    spread = jnp.where(lane // TOPK == token, final[line : line + 1, features:], 0.0)
    choose = (
        lax.broadcasted_iota(jnp.int32, (TOPK, LANES), 1) % TOPK
        == lax.broadcasted_iota(jnp.int32, (TOPK, LANES), 0)
    ).astype(F32)
    route_ref[...] = lax.dot_general(
        choose, spread, NT, precision=lax.Precision.HIGHEST, preferred_element_type=F32
    )


def finish(total, parts, term):
    tokens, features = term.shape
    return pl.pallas_call(
        finish_kernel,
        out_shape=[
            jax.ShapeDtypeStruct((tokens, features), BF16),
            jax.ShapeDtypeStruct((TOPK, tokens), F32),
            jax.ShapeDtypeStruct((features // LANES, LANES), F32),
        ],
        compiler_params=pltpu.CompilerParams(vmem_limit_bytes=4 << 20),
        name="finish",
    )(total, *parts, term)


def square_device(
    norm_input, out_grad, shared_out, expert_ids, route_weight, shared_gate, w_gate, w_up, w_down
):
    tokens, features = norm_input.shape
    sources = lax.axis_size("expert")
    mine = pack(norm_input, out_grad, expert_ids, route_weight)
    tail, term = shared(norm_input, out_grad, shared_out, shared_gate)
    held = [mine] + [swap(mine, "expert", d) for d in range(1, sources)]
    held[2], tail, term = lax.optimization_barrier((held[2], tail, term))
    held = held + [swap(block, "dp", 2) for block in held]
    held = held + [swap(block, "dp", 1) for block in held]
    kept, sent = run_experts(held, tail, w_gate, w_up, w_down, sources)
    total = (kept.astype(F32) + swap(sent, "dp", 1).astype(F32)).astype(BF16)
    half = total.shape[0] // 2
    total = (total[:half].astype(F32) + swap(total[half:], "dp", 2).astype(F32)).astype(BF16)
    parts = [
        swap(total[d * tokens : (d + 1) * tokens], "expert", d) for d in range(sources - 1, 0, -1)
    ]
    input_grad, route_grad, gate_grad = finish(total, parts, term)
    return (input_grad, route_grad.T, gate_grad.reshape(features))


def solution(mesh):
    square = mesh.shape["expert"] == 4 and mesh.shape["dp"] == 4
    on_device = square_device if square else general_device
    return jax.shard_map(
        on_device,
        mesh=mesh,
        in_specs=(
            P(("groups", "expert", "dp"), None),
            P(("groups", "expert", "dp"), None),
            P(("groups", "expert", "dp"), None),
            P(("groups", "expert", "dp"), None),
            P(("groups", "expert", "dp"), None),
            P(),
            P("expert", None, "dp"),
            P("expert", None, "dp"),
            P("expert", "dp", None),
        ),
        out_specs=(
            P(("groups", "expert", "dp"), None),
            P(("groups", "expert", "dp"), None),
            P("groups"),
        ),
        check_vma=False,
    )
```

```python
import functools

import jax
import jax.numpy as jnp
import numpy as np
from jax import lax
from jax.experimental import pallas as pl
from jax.experimental.pallas import tpu as pltpu
from jax.sharding import PartitionSpec as P

EXPERTS = 64
TOPK = 8
CAP = 12
LANES = 128
BF16 = jnp.bfloat16
F32 = jnp.float32
NT = (((1,), (1,)), ((), ()))
TN = (((0,), (0,)), ((), ()))


def slot_targets(group_ids):
    flat_ids = group_ids.reshape(-1)
    one_hot = (flat_ids[:, None] == jnp.arange(EXPERTS, dtype=jnp.int32)[None, :]).astype(jnp.int32)
    before = jnp.cumsum(one_hot, axis=0) - one_hot
    position = jnp.sum(before * one_hot, axis=1)
    return flat_ids * CAP + position


def general_device(
    norm_input, out_grad, shared_out, expert_ids, route_weight, shared_gate, w_gate, w_up, w_down
):
    features = norm_input.shape[1]
    group_norm, group_grad, group_codes, group_weight = (
        lax.all_gather(norm_input, "dp", axis=0, tiled=True),
        lax.all_gather(out_grad, "dp", axis=0, tiled=True),
        lax.all_gather(expert_ids.astype(jnp.bfloat16), "dp", axis=0, tiled=True),
        lax.all_gather(route_weight, "dp", axis=0, tiled=True),
    )
    group_ids = group_codes.astype(jnp.int32)
    group_tokens = group_norm.shape[0]
    target = slot_targets(group_ids)
    slots = jnp.arange(EXPERTS * CAP, dtype=jnp.int32)
    hits = (target[None, :] == slots[:, None]).astype(jnp.bfloat16)
    dispatch = hits.reshape(EXPERTS * CAP, group_tokens, TOPK).sum(axis=2)
    slot_norm = jnp.dot(dispatch, group_norm, preferred_element_type=jnp.float32).astype(
        jnp.bfloat16
    )
    slot_grad = jnp.dot(dispatch, group_grad, preferred_element_type=jnp.float32).astype(
        jnp.bfloat16
    )
    slot_norm = slot_norm.reshape(EXPERTS, CAP, features)
    slot_grad = slot_grad.reshape(EXPERTS, CAP, features)
    local_experts = w_gate.shape[0]
    quarter = CAP // lax.axis_size("dp")
    offset = lax.axis_index("dp") * quarter
    norm_share = lax.dynamic_slice_in_dim(slot_norm, offset, quarter, 1)
    grad_share = lax.dynamic_slice_in_dim(slot_grad, offset, quarter, 1)
    arrived_norm, arrived_grad = (
        lax.all_to_all(norm_share, "expert", split_axis=0, concat_axis=0, tiled=True),
        lax.all_to_all(grad_share, "expert", split_axis=0, concat_axis=0, tiled=True),
    )
    rows_in = lax.all_gather(arrived_norm, "dp", axis=1, tiled=True)
    grads_in = lax.all_gather(arrived_grad, "dp", axis=1, tiled=True)
    item_count = rows_in.shape[1]
    sources = rows_in.shape[0] // local_experts
    rows_four = rows_in.reshape(sources, local_experts, item_count, features)
    grads_four = grads_in.reshape(sources, local_experts, item_count, features)
    gate_pre = jnp.einsum("sxcd,xdf->sxcf", rows_four, w_gate, preferred_element_type=jnp.float32)
    up_pre = jnp.einsum("sxcd,xdf->sxcf", rows_four, w_up, preferred_element_type=jnp.float32)
    hidden_grad = jnp.einsum(
        "sxcd,xfd->sxcf", grads_four, w_down, preferred_element_type=jnp.float32
    )
    logistic = jax.nn.sigmoid(gate_pre)
    swish = gate_pre * logistic
    act = swish * up_pre
    gate_diff = (hidden_grad * up_pre * logistic * (1.0 + gate_pre * (1.0 - logistic))).astype(
        jnp.bfloat16
    )
    up_diff = (hidden_grad * swish).astype(jnp.bfloat16)
    row_part = jnp.einsum("sxcf,xdf->sxcd", gate_diff, w_gate, preferred_element_type=jnp.float32)
    row_part = row_part + jnp.einsum(
        "sxcf,xdf->sxcd", up_diff, w_up, preferred_element_type=jnp.float32
    )
    row_back = row_part.astype(jnp.bfloat16).reshape(sources * local_experts, item_count, features)
    score_back = jnp.sum(act * hidden_grad, axis=3).astype(jnp.bfloat16)
    score_back = score_back.reshape(sources * local_experts, item_count, 1)
    back_rows = lax.all_to_all(row_back, "expert", split_axis=0, concat_axis=0, tiled=True)
    back_scores = lax.all_to_all(score_back, "expert", split_axis=0, concat_axis=0, tiled=True)
    columns = back_rows.shape[2]
    back_flat = back_rows.reshape(EXPERTS * CAP, columns)
    score_flat = back_scores.reshape(EXPERTS * CAP)
    picked = jnp.take(back_flat, target, axis=0).reshape(group_tokens, TOPK, columns)
    token_part = jnp.einsum(
        "tk,tkd->td", group_weight.astype(jnp.float32), picked.astype(jnp.float32)
    )
    score_part = (
        jnp.take(score_flat, target, axis=0).astype(jnp.float32).reshape(group_tokens, TOPK)
    )
    routed, route_grad = (
        lax.psum_scatter(
            token_part.astype(jnp.bfloat16), "dp", scatter_dimension=0, tiled=True
        ).astype(jnp.float32),
        lax.psum_scatter(
            score_part.astype(jnp.bfloat16), "dp", scatter_dimension=0, tiled=True
        ).astype(jnp.float32),
    )
    gate_value = jax.nn.sigmoid(
        jnp.dot(norm_input, shared_gate, preferred_element_type=jnp.float32)
    )
    inner = jnp.sum(out_grad.astype(jnp.float32) * shared_out.astype(jnp.float32), axis=1)
    gate_delta = inner * gate_value * (1.0 - gate_value)
    input_grad = (routed + gate_delta[:, None] * shared_gate.astype(jnp.float32)[None, :]).astype(
        jnp.bfloat16
    )
    gate_local = jnp.dot(
        gate_delta, norm_input.astype(jnp.float32), precision=lax.Precision.HIGHEST
    )
    gate_grad = lax.psum(gate_local, ("expert", "dp"))
    return (input_grad, route_grad, gate_grad)


def dot(a, b, dims=(((1,), (0,)), ((), ()))):
    return lax.dot_general(a, b, dims, preferred_element_type=F32)


def swap(value, axis, distance):
    size = lax.axis_size(axis)
    return lax.ppermute(value, axis, [(i, i ^ distance) for i in range(size)])


def experts_kernel(features, rows, blocks, group, *refs):
    token_refs, refs = refs[:blocks], refs[blocks:]
    tail_ref, w_gate, w_up, w_down, keep_ref, send_ref, tokens, copied, gates, ups, downs, loaded, spread, weighted, norms, grads, backs, hits, routes = refs
    number = w_gate.shape[0]
    starts = np.cumsum([0] + [ref.shape[0] for ref in token_refs])
    count = int(starts[-1])

    def loads(turn, k):
        expert = turn * group + k
        slot = lax.rem(turn, 3) * group + k
        return [
            pltpu.make_async_copy(source.at[expert], target.at[slot], loaded.at[slot, j])
            for j, (source, target) in enumerate(((w_gate, gates), (w_up, ups), (w_down, downs)))
        ]

    copies = [
        pltpu.make_async_copy(ref, tokens.at[pl.ds(int(starts[j]), ref.shape[0])], copied.at[j])
        for j, ref in enumerate(token_refs)
    ]
    for copy in copies:
        copy.start()
    for k in range(group):
        for copy in loads(0, k):
            copy.start()
    for copy in copies:
        copy.wait()
    for k in range(group):
        for copy in loads(1, k):
            copy.start()
    codes = tokens[:, 2 * features :].astype(F32).T
    weights = codes[TOPK : 2 * TOPK]
    local = codes[:TOPK] - (lax.axis_index("expert") * number).astype(F32)
    hits[...] = local
    earlier = (
        lax.broadcasted_iota(jnp.int32, (count, count), 0)
        < lax.broadcasted_iota(jnp.int32, (count, count), 1)
    ).astype(BF16)
    masks = [local == float(e) for e in range(number)]
    member = jnp.concatenate(
        [jnp.sum(m.astype(F32), axis=0, keepdims=True) for m in masks], axis=0
    )
    position = dot(member.astype(BF16), earlier)
    slot = lax.broadcasted_iota(jnp.int32, (rows, count), 0).astype(F32)
    for e in range(number):
        weight = jnp.sum(jnp.where(masks[e], weights, 0.0), axis=0, keepdims=True)
        chosen = (slot == position[e : e + 1]) & (member[e : e + 1] > 0.0)
        spread[e * rows : (e + 1) * rows] = jnp.where(chosen, 1.0, 0.0).astype(BF16)
        weighted[e * rows : (e + 1) * rows] = jnp.where(chosen, weight, 0.0).astype(BF16)
    norms[...] = dot(spread[...], tokens[:, :features]).astype(BF16)
    grads[...] = dot(spread[...], tokens[:, features : 2 * features]).astype(BF16)
    routes[...] = jnp.zeros_like(routes)

    def run(turn, _):
        base = lax.rem(turn, 3) * group
        heres = [
            pl.ds(pl.multiple_of((turn * group + k) * rows, rows), rows) for k in range(group)
        ]
        for k in range(group):
            for copy in loads(turn, k):
                copy.wait()
        @pl.when(turn + 2 < number // group)
        def _():
            for k in range(group):
                for copy in loads(turn + 2, k):
                    copy.start()

        pre = []
        for k in range(group):
            x, dy = norms[heres[k]], grads[heres[k]]
            pre.append((dot(x, gates[base + k]), dot(x, ups[base + k]), dot(dy, downs[base + k], NT)))
        for k in range(group):
            gate_pre, up_pre, hidden_grad = pre[k]
            logistic = jax.nn.sigmoid(gate_pre)
            swish = gate_pre * logistic
            gate_diff = (
                hidden_grad * up_pre * logistic * (1.0 + gate_pre * (1.0 - logistic))
            ).astype(BF16)
            up_diff = (hidden_grad * swish).astype(BF16)
            first_part = dot(gate_diff, gates[base + k], NT)
            second_part = dot(ups[base + k], up_diff, NT).T
            backs[heres[k]] = (first_part + second_part).astype(BF16)
            score = jnp.sum(swish * up_pre * hidden_grad, axis=1, keepdims=True)
            by_token = jnp.sum(spread[heres[k]].astype(F32) * score, axis=0, keepdims=True)
            here = (turn * group + k).astype(F32)
            routes[...] += jnp.where(hits[...] == here, by_token, 0.0)

        return 0

    lax.fori_loop(0, number // group, run, 0)
    half = count // 2
    result = dot(weighted[...], backs[...], TN).astype(BF16)
    each = tail_ref.shape[0]
    line = features // LANES
    token = lax.broadcasted_iota(jnp.int32, (count, LANES), 0)
    lane = lax.broadcasted_iota(jnp.int32, (count, LANES), 1)
    repeat = (
        lax.broadcasted_iota(jnp.int32, (TOPK, LANES), 1) % TOPK
        == lax.broadcasted_iota(jnp.int32, (TOPK, LANES), 0)
    ).astype(BF16)
    scores = dot(routes[...].astype(BF16), repeat, TN)
    scores = jnp.where(lane // TOPK == token % each, scores, 0.0).astype(BF16)
    row = lax.broadcasted_iota(jnp.int32, (count, count), 0)
    column = lax.broadcasted_iota(jnp.int32, (count, count), 1)
    gather = ((row % each == line) & (row // each == column // each)).astype(BF16)
    tail = jnp.concatenate([tail_ref[...]] * (count // each), axis=0)
    last = (dot(gather, scores) + tail).astype(BF16)
    keep_ref[:, :features] = result[:half]
    send_ref[:, :features] = result[half:]
    keep_ref[:, features:] = last[:half]
    send_ref[:, features:] = last[half:]


def run_experts(token_blocks, tail, w_gate, w_up, w_down, sources):
    local, features, hidden = w_gate.shape
    blocks = len(token_blocks)
    count = sum(block.shape[0] for block in token_blocks)
    rows = sources * CAP
    width = features + LANES
    group = 2
    away = pl.BlockSpec(memory_space=pl.ANY)
    near = pl.BlockSpec(memory_space=pltpu.VMEM)
    return pl.pallas_call(
        functools.partial(experts_kernel, features, rows, blocks, group),
        in_specs=[away] * blocks + [near, away, away, away],
        out_specs=[near] * 2,
        out_shape=[jax.ShapeDtypeStruct((count // 2, width), BF16)] * 2,
        scratch_shapes=[
            pltpu.VMEM((count, 2 * features + LANES), BF16),
            pltpu.SemaphoreType.DMA((blocks,)),
            pltpu.VMEM((3 * group, features, hidden), BF16),
            pltpu.VMEM((3 * group, features, hidden), BF16),
            pltpu.VMEM((3 * group, hidden, features), BF16),
            pltpu.SemaphoreType.DMA((3 * group, 3)),
            pltpu.VMEM((local * rows, count), BF16),
            pltpu.VMEM((local * rows, count), BF16),
            pltpu.VMEM((local * rows, features), BF16),
            pltpu.VMEM((local * rows, features), BF16),
            pltpu.VMEM((local * rows, features), BF16),
            pltpu.VMEM((TOPK, count), F32),
            pltpu.VMEM((TOPK, count), F32),
        ],
        compiler_params=pltpu.CompilerParams(vmem_limit_bytes=44 << 20),
        name="experts",
    )(*token_blocks, tail, w_gate, w_up, w_down)


def in_hbm(value):
    return pltpu.with_memory_space_constraint(value, pltpu.HBM)


def pack_kernel(norm_ref, grad_ref, ids_ref, weight_ref, packed_ref, copied):
    features = norm_ref.shape[1]
    copies = [
        pltpu.make_async_copy(ref, packed_ref.at[:, pl.ds(j * features, features)], copied.at[j])
        for j, ref in enumerate((norm_ref, grad_ref))
    ]
    for copy in copies:
        copy.start()
    lane = lax.broadcasted_iota(jnp.int32, (TOPK, LANES), 1)
    source = lax.broadcasted_iota(jnp.int32, (TOPK, LANES), 0)
    ids = ids_ref[...].astype(F32).astype(BF16)
    codes = dot(ids, (lane == source).astype(BF16), TN) + dot(
        weight_ref[...], (lane == source + TOPK).astype(BF16), TN
    )
    packed_ref[:, 2 * features :] = codes.astype(BF16)
    for copy in copies:
        copy.wait()


def pack(norm_input, out_grad, expert_ids, route_weight):
    tokens, features = norm_input.shape
    away = pl.BlockSpec(memory_space=pltpu.HBM)
    near = pl.BlockSpec(memory_space=pltpu.VMEM)
    return pl.pallas_call(
        pack_kernel,
        in_specs=[away, away, near, near],
        out_specs=near,
        out_shape=jax.ShapeDtypeStruct((tokens, 2 * features + LANES), BF16),
        scratch_shapes=[pltpu.SemaphoreType.DMA((2,))],
        compiler_params=pltpu.CompilerParams(vmem_limit_bytes=4 << 20),
        name="pack",
    )(*map(in_hbm, (norm_input, out_grad, expert_ids.T, route_weight.T)))


def shared_kernel(norm_ref, grad_ref, shared_ref, gate_ref, tail_ref, term_ref, copied, norms, grads, outs):
    features = norm_ref.shape[1]
    copies = [
        pltpu.make_async_copy(ref, target, copied.at[j])
        for j, (ref, target) in enumerate(((norm_ref, norms), (grad_ref, grads), (shared_ref, outs)))
    ]
    for copy in copies:
        copy.start()
    for copy in copies:
        copy.wait()
    norm = norms[...].astype(F32)
    gate = gate_ref[...].astype(F32)
    gate_value = jax.nn.sigmoid(jnp.sum(norm * gate, axis=1, keepdims=True))
    inner = jnp.sum(grads[...].astype(F32) * outs[...].astype(F32), axis=1, keepdims=True)
    delta = inner * gate_value * (1.0 - gate_value)
    term_ref[...] = delta * gate
    local = jnp.sum(delta * norm, axis=0, keepdims=True)
    tail_ref[...] = jnp.zeros_like(tail_ref)
    for r in range(features // LANES):
        tail_ref[r : r + 1, :] = local[:, r * LANES : (r + 1) * LANES]


def shared(norm_input, out_grad, shared_out, shared_gate):
    tokens, features = norm_input.shape
    away = pl.BlockSpec(memory_space=pltpu.HBM)
    near = pl.BlockSpec(memory_space=pltpu.VMEM)
    return pl.pallas_call(
        shared_kernel,
        in_specs=[away, away, away, near],
        out_specs=[near, near],
        out_shape=[
            jax.ShapeDtypeStruct((tokens, LANES), F32),
            jax.ShapeDtypeStruct((tokens, features), F32),
        ],
        scratch_shapes=[pltpu.SemaphoreType.DMA((3,))]
        + [pltpu.VMEM((tokens, features), BF16)] * 3,
        compiler_params=pltpu.CompilerParams(vmem_limit_bytes=4 << 20),
        name="shared",
    )(*map(in_hbm, (norm_input, out_grad, shared_out)), shared_gate[None, :])


def finish_kernel(total_ref, *refs):
    parts, (term_ref, input_ref, route_ref, gate_ref) = refs[:-4], refs[-4:]
    tokens, features = term_ref.shape
    final = total_ref[:tokens].astype(F32)
    for part in parts:
        final = final + part[:tokens].astype(F32)
    input_ref[...] = (final[:, :features] + term_ref[...]).astype(BF16)
    line = features // LANES
    gate_ref[...] = final[:line, features:]
    lane = lax.broadcasted_iota(jnp.int32, (tokens, LANES), 1)
    token = lax.broadcasted_iota(jnp.int32, (tokens, LANES), 0)
    spread = jnp.where(lane // TOPK == token, final[line : line + 1, features:], 0.0)
    choose = (
        lax.broadcasted_iota(jnp.int32, (TOPK, LANES), 1) % TOPK
        == lax.broadcasted_iota(jnp.int32, (TOPK, LANES), 0)
    ).astype(F32)
    route_ref[...] = lax.dot_general(
        choose, spread, NT, precision=lax.Precision.HIGHEST, preferred_element_type=F32
    )


def finish(total, parts, term):
    tokens, features = term.shape
    return pl.pallas_call(
        finish_kernel,
        out_shape=[
            jax.ShapeDtypeStruct((tokens, features), BF16),
            jax.ShapeDtypeStruct((TOPK, tokens), F32),
            jax.ShapeDtypeStruct((features // LANES, LANES), F32),
        ],
        compiler_params=pltpu.CompilerParams(vmem_limit_bytes=4 << 20),
        name="finish",
    )(total, *parts, term)


def add(a, b):
    return (a.astype(F32) + b.astype(F32)).astype(BF16)


def square_device(
    norm_input, out_grad, shared_out, expert_ids, route_weight, shared_gate, w_gate, w_up, w_down
):
    tokens, features = norm_input.shape
    sources = lax.axis_size("expert")
    mine = pack(norm_input, out_grad, expert_ids, route_weight)
    tail, term = shared(norm_input, out_grad, shared_out, shared_gate)
    x0 = swap(mine, "dp", 2)
    z1 = swap(mine, "expert", 1)
    z2 = swap(mine, "expert", 2)
    z3 = swap(z2, "expert", 1)
    z3, tail, term = lax.optimization_barrier((z3, tail, term))
    xz1 = swap(z1, "dp", 2)
    xz2 = swap(z2, "dp", 2)
    xz3 = swap(xz2, "expert", 1)
    held = [mine, z1, z2, z3, x0, xz1, xz2, xz3]
    held = held + [swap(block, "dp", 1) for block in held]
    kept, sent = run_experts(held, tail, w_gate, w_up, w_down, sources)
    total = (kept.astype(F32) + swap(sent, "dp", 1).astype(F32)).astype(BF16)
    own = [total[j * tokens : (j + 1) * tokens] for j in range(2 * sources)]
    far = swap(jnp.concatenate([own[3], own[7]], axis=0), "expert", 1)
    near = swap(total[4 * tokens : 6 * tokens], "dp", 2)
    third = swap(add(own[6], far[tokens:]), "dp", 2)
    second = swap(add(own[1], near[tokens:]), "expert", 1)
    fourth = swap(add(add(own[2], far[:tokens]), third), "expert", 2)
    parts = [near, second, fourth]
    input_grad, route_grad, gate_grad = finish(total, parts, term)
    return (input_grad, route_grad.T, gate_grad.reshape(features))


def solution(mesh):
    square = mesh.shape["expert"] == 4 and mesh.shape["dp"] == 4
    on_device = square_device if square else general_device
    return jax.shard_map(
        on_device,
        mesh=mesh,
        in_specs=(
            P(("groups", "expert", "dp"), None),
            P(("groups", "expert", "dp"), None),
            P(("groups", "expert", "dp"), None),
            P(("groups", "expert", "dp"), None),
            P(("groups", "expert", "dp"), None),
            P(),
            P("expert", None, "dp"),
            P("expert", None, "dp"),
            P("expert", "dp", None),
        ),
        out_specs=(
            P(("groups", "expert", "dp"), None),
            P(("groups", "expert", "dp"), None),
            P("groups"),
        ),
        check_vma=False,
    )
```

```python
import functools

import jax
import jax.numpy as jnp
import numpy as np
from jax import lax
from jax.experimental import pallas as pl
from jax.experimental.pallas import tpu as pltpu
from jax.sharding import PartitionSpec as P

EXPERTS = 64
TOPK = 8
CAP = 12
LANES = 128
BF16 = jnp.bfloat16
F32 = jnp.float32
NT = (((1,), (1,)), ((), ()))
TN = (((0,), (0,)), ((), ()))


def slot_targets(group_ids):
    flat_ids = group_ids.reshape(-1)
    one_hot = (flat_ids[:, None] == jnp.arange(EXPERTS, dtype=jnp.int32)[None, :]).astype(jnp.int32)
    before = jnp.cumsum(one_hot, axis=0) - one_hot
    position = jnp.sum(before * one_hot, axis=1)
    return flat_ids * CAP + position


def general_device(
    norm_input, out_grad, shared_out, expert_ids, route_weight, shared_gate, w_gate, w_up, w_down
):
    features = norm_input.shape[1]
    group_norm, group_grad, group_codes, group_weight = (
        lax.all_gather(norm_input, "dp", axis=0, tiled=True),
        lax.all_gather(out_grad, "dp", axis=0, tiled=True),
        lax.all_gather(expert_ids.astype(jnp.bfloat16), "dp", axis=0, tiled=True),
        lax.all_gather(route_weight, "dp", axis=0, tiled=True),
    )
    group_ids = group_codes.astype(jnp.int32)
    group_tokens = group_norm.shape[0]
    target = slot_targets(group_ids)
    slots = jnp.arange(EXPERTS * CAP, dtype=jnp.int32)
    hits = (target[None, :] == slots[:, None]).astype(jnp.bfloat16)
    dispatch = hits.reshape(EXPERTS * CAP, group_tokens, TOPK).sum(axis=2)
    slot_norm = jnp.dot(dispatch, group_norm, preferred_element_type=jnp.float32).astype(
        jnp.bfloat16
    )
    slot_grad = jnp.dot(dispatch, group_grad, preferred_element_type=jnp.float32).astype(
        jnp.bfloat16
    )
    slot_norm = slot_norm.reshape(EXPERTS, CAP, features)
    slot_grad = slot_grad.reshape(EXPERTS, CAP, features)
    local_experts = w_gate.shape[0]
    quarter = CAP // lax.axis_size("dp")
    offset = lax.axis_index("dp") * quarter
    norm_share = lax.dynamic_slice_in_dim(slot_norm, offset, quarter, 1)
    grad_share = lax.dynamic_slice_in_dim(slot_grad, offset, quarter, 1)
    arrived_norm, arrived_grad = (
        lax.all_to_all(norm_share, "expert", split_axis=0, concat_axis=0, tiled=True),
        lax.all_to_all(grad_share, "expert", split_axis=0, concat_axis=0, tiled=True),
    )
    rows_in = lax.all_gather(arrived_norm, "dp", axis=1, tiled=True)
    grads_in = lax.all_gather(arrived_grad, "dp", axis=1, tiled=True)
    item_count = rows_in.shape[1]
    sources = rows_in.shape[0] // local_experts
    rows_four = rows_in.reshape(sources, local_experts, item_count, features)
    grads_four = grads_in.reshape(sources, local_experts, item_count, features)
    gate_pre = jnp.einsum("sxcd,xdf->sxcf", rows_four, w_gate, preferred_element_type=jnp.float32)
    up_pre = jnp.einsum("sxcd,xdf->sxcf", rows_four, w_up, preferred_element_type=jnp.float32)
    hidden_grad = jnp.einsum(
        "sxcd,xfd->sxcf", grads_four, w_down, preferred_element_type=jnp.float32
    )
    logistic = jax.nn.sigmoid(gate_pre)
    swish = gate_pre * logistic
    act = swish * up_pre
    gate_diff = (hidden_grad * up_pre * logistic * (1.0 + gate_pre * (1.0 - logistic))).astype(
        jnp.bfloat16
    )
    up_diff = (hidden_grad * swish).astype(jnp.bfloat16)
    row_part = jnp.einsum("sxcf,xdf->sxcd", gate_diff, w_gate, preferred_element_type=jnp.float32)
    row_part = row_part + jnp.einsum(
        "sxcf,xdf->sxcd", up_diff, w_up, preferred_element_type=jnp.float32
    )
    row_back = row_part.astype(jnp.bfloat16).reshape(sources * local_experts, item_count, features)
    score_back = jnp.sum(act * hidden_grad, axis=3).astype(jnp.bfloat16)
    score_back = score_back.reshape(sources * local_experts, item_count, 1)
    back_rows = lax.all_to_all(row_back, "expert", split_axis=0, concat_axis=0, tiled=True)
    back_scores = lax.all_to_all(score_back, "expert", split_axis=0, concat_axis=0, tiled=True)
    columns = back_rows.shape[2]
    back_flat = back_rows.reshape(EXPERTS * CAP, columns)
    score_flat = back_scores.reshape(EXPERTS * CAP)
    picked = jnp.take(back_flat, target, axis=0).reshape(group_tokens, TOPK, columns)
    token_part = jnp.einsum(
        "tk,tkd->td", group_weight.astype(jnp.float32), picked.astype(jnp.float32)
    )
    score_part = (
        jnp.take(score_flat, target, axis=0).astype(jnp.float32).reshape(group_tokens, TOPK)
    )
    routed, route_grad = (
        lax.psum_scatter(
            token_part.astype(jnp.bfloat16), "dp", scatter_dimension=0, tiled=True
        ).astype(jnp.float32),
        lax.psum_scatter(
            score_part.astype(jnp.bfloat16), "dp", scatter_dimension=0, tiled=True
        ).astype(jnp.float32),
    )
    gate_value = jax.nn.sigmoid(
        jnp.dot(norm_input, shared_gate, preferred_element_type=jnp.float32)
    )
    inner = jnp.sum(out_grad.astype(jnp.float32) * shared_out.astype(jnp.float32), axis=1)
    gate_delta = inner * gate_value * (1.0 - gate_value)
    input_grad = (routed + gate_delta[:, None] * shared_gate.astype(jnp.float32)[None, :]).astype(
        jnp.bfloat16
    )
    gate_local = jnp.dot(
        gate_delta, norm_input.astype(jnp.float32), precision=lax.Precision.HIGHEST
    )
    gate_grad = lax.psum(gate_local, ("expert", "dp"))
    return (input_grad, route_grad, gate_grad)


def dot(a, b, dims=(((1,), (0,)), ((), ()))):
    return lax.dot_general(a, b, dims, preferred_element_type=F32)


def swap(value, axis, distance):
    size = lax.axis_size(axis)
    return lax.ppermute(value, axis, [(i, i ^ distance) for i in range(size)])


def experts_kernel(features, rows, blocks, group, *refs):
    token_refs, refs = refs[:blocks], refs[blocks:]
    tail_ref, w_gate, w_up, w_down, keep_ref, send_ref, gates, ups, downs, loaded, spread, weighted, norms, grads, backs, hits, routes = refs
    number = w_gate.shape[0]
    starts = np.cumsum([0] + [ref.shape[0] for ref in token_refs])
    count = int(starts[-1])

    def loads(turn, k):
        expert = turn * group + k
        slot = lax.rem(turn, 3) * group + k
        return [
            pltpu.make_async_copy(source.at[expert], target.at[slot], loaded.at[slot, j])
            for j, (source, target) in enumerate(((w_gate, gates), (w_up, ups), (w_down, downs)))
        ]

    for k in range(group):
        for copy in loads(0, k):
            copy.start()
    def together(columns):
        return jnp.concatenate([ref[:, columns] for ref in token_refs], axis=0)

    codes = together(slice(2 * features, None)).astype(F32).T
    weights = codes[TOPK : 2 * TOPK]
    local = codes[:TOPK] - (lax.axis_index("expert") * number).astype(F32)
    hits[...] = local
    earlier = (
        lax.broadcasted_iota(jnp.int32, (count, count), 0)
        < lax.broadcasted_iota(jnp.int32, (count, count), 1)
    ).astype(BF16)
    masks = [local == float(e) for e in range(number)]
    member = jnp.concatenate(
        [jnp.sum(m.astype(F32), axis=0, keepdims=True) for m in masks], axis=0
    )
    position = dot(member.astype(BF16), earlier)
    slot = lax.broadcasted_iota(jnp.int32, (rows, count), 0).astype(F32)
    for e in range(number):
        weight = jnp.sum(jnp.where(masks[e], weights, 0.0), axis=0, keepdims=True)
        chosen = (slot == position[e : e + 1]) & (member[e : e + 1] > 0.0)
        spread[e * rows : (e + 1) * rows] = jnp.where(chosen, 1.0, 0.0).astype(BF16)
        weighted[e * rows : (e + 1) * rows] = jnp.where(chosen, weight, 0.0).astype(BF16)
    for k in range(group):
        for copy in loads(1, k):
            copy.start()
    norms[...] = dot(spread[...], together(slice(0, features))).astype(BF16)
    grads[...] = dot(spread[...], together(slice(features, 2 * features))).astype(BF16)
    routes[...] = jnp.zeros_like(routes)

    def run(turn, _):
        base = lax.rem(turn, 3) * group
        heres = [
            pl.ds(pl.multiple_of((turn * group + k) * rows, rows), rows) for k in range(group)
        ]
        for k in range(group):
            for copy in loads(turn, k):
                copy.wait()
        @pl.when(turn + 2 < number // group)
        def _():
            for k in range(group):
                for copy in loads(turn + 2, k):
                    copy.start()

        pre = []
        for k in range(group):
            x, dy = norms[heres[k]], grads[heres[k]]
            pre.append((dot(x, gates[base + k]), dot(x, ups[base + k]), dot(dy, downs[base + k], NT)))
        for k in range(group):
            gate_pre, up_pre, hidden_grad = pre[k]
            logistic = jax.nn.sigmoid(gate_pre)
            swish = gate_pre * logistic
            gate_diff = (
                hidden_grad * up_pre * logistic * (1.0 + gate_pre * (1.0 - logistic))
            ).astype(BF16)
            up_diff = (hidden_grad * swish).astype(BF16)
            first_part = dot(gate_diff, gates[base + k], NT)
            second_part = dot(ups[base + k], up_diff, NT).T
            backs[heres[k]] = (first_part + second_part).astype(BF16)
            score = jnp.sum(swish * up_pre * hidden_grad, axis=1, keepdims=True)
            by_token = jnp.sum(spread[heres[k]].astype(F32) * score, axis=0, keepdims=True)
            here = (turn * group + k).astype(F32)
            routes[...] += jnp.where(hits[...] == here, by_token, 0.0)

        return 0

    lax.fori_loop(0, number // group, run, 0)
    half = count // 2
    result = dot(weighted[...], backs[...], TN).astype(BF16)
    each = tail_ref.shape[0]
    line = features // LANES
    token = lax.broadcasted_iota(jnp.int32, (count, LANES), 0)
    lane = lax.broadcasted_iota(jnp.int32, (count, LANES), 1)
    repeat = (
        lax.broadcasted_iota(jnp.int32, (TOPK, LANES), 1) % TOPK
        == lax.broadcasted_iota(jnp.int32, (TOPK, LANES), 0)
    ).astype(BF16)
    scores = dot(routes[...].astype(BF16), repeat, TN)
    scores = jnp.where(lane // TOPK == token % each, scores, 0.0).astype(BF16)
    row = lax.broadcasted_iota(jnp.int32, (count, count), 0)
    column = lax.broadcasted_iota(jnp.int32, (count, count), 1)
    gather = ((row % each == line) & (row // each == column // each)).astype(BF16)
    tail = jnp.concatenate([tail_ref[...]] * (count // each), axis=0)
    last = (dot(gather, scores) + tail).astype(BF16)
    keep_ref[:, :features] = result[:half]
    send_ref[:, :features] = result[half:]
    keep_ref[:, features:] = last[:half]
    send_ref[:, features:] = last[half:]


def run_experts(token_blocks, tail, w_gate, w_up, w_down, sources):
    local, features, hidden = w_gate.shape
    blocks = len(token_blocks)
    count = sum(block.shape[0] for block in token_blocks)
    rows = sources * CAP
    width = features + LANES
    group = 2
    away = pl.BlockSpec(memory_space=pl.ANY)
    near = pl.BlockSpec(memory_space=pltpu.VMEM)
    return pl.pallas_call(
        functools.partial(experts_kernel, features, rows, blocks, group),
        in_specs=[near] * (blocks + 1) + [away] * 3,
        out_specs=[near] * 2,
        out_shape=[jax.ShapeDtypeStruct((count // 2, width), BF16)] * 2,
        scratch_shapes=[
            pltpu.VMEM((3 * group, features, hidden), BF16),
            pltpu.VMEM((3 * group, features, hidden), BF16),
            pltpu.VMEM((3 * group, hidden, features), BF16),
            pltpu.SemaphoreType.DMA((3 * group, 3)),
            pltpu.VMEM((local * rows, count), BF16),
            pltpu.VMEM((local * rows, count), BF16),
            pltpu.VMEM((local * rows, features), BF16),
            pltpu.VMEM((local * rows, features), BF16),
            pltpu.VMEM((local * rows, features), BF16),
            pltpu.VMEM((TOPK, count), F32),
            pltpu.VMEM((TOPK, count), F32),
        ],
        compiler_params=pltpu.CompilerParams(vmem_limit_bytes=44 << 20),
        name="experts",
    )(*token_blocks, tail, w_gate, w_up, w_down)


def in_hbm(value):
    return pltpu.with_memory_space_constraint(value, pltpu.HBM)


def pack_kernel(norm_ref, grad_ref, ids_ref, weight_ref, packed_ref, copied):
    features = norm_ref.shape[1]
    copies = [
        pltpu.make_async_copy(ref, packed_ref.at[:, pl.ds(j * features, features)], copied.at[j])
        for j, ref in enumerate((norm_ref, grad_ref))
    ]
    for copy in copies:
        copy.start()
    lane = lax.broadcasted_iota(jnp.int32, (TOPK, LANES), 1)
    source = lax.broadcasted_iota(jnp.int32, (TOPK, LANES), 0)
    ids = ids_ref[...].astype(F32).astype(BF16)
    codes = dot(ids, (lane == source).astype(BF16), TN) + dot(
        weight_ref[...], (lane == source + TOPK).astype(BF16), TN
    )
    packed_ref[:, 2 * features :] = codes.astype(BF16)
    for copy in copies:
        copy.wait()


def pack(norm_input, out_grad, expert_ids, route_weight):
    tokens, features = norm_input.shape
    away = pl.BlockSpec(memory_space=pltpu.HBM)
    near = pl.BlockSpec(memory_space=pltpu.VMEM)
    return pl.pallas_call(
        pack_kernel,
        in_specs=[away, away, near, near],
        out_specs=near,
        out_shape=jax.ShapeDtypeStruct((tokens, 2 * features + LANES), BF16),
        scratch_shapes=[pltpu.SemaphoreType.DMA((2,))],
        compiler_params=pltpu.CompilerParams(vmem_limit_bytes=4 << 20),
        name="pack",
    )(*map(in_hbm, (norm_input, out_grad, expert_ids.T, route_weight.T)))


def shared_kernel(norm_ref, grad_ref, shared_ref, gate_ref, tail_ref, term_ref, copied, norms, grads, outs):
    features = norm_ref.shape[1]
    copies = [
        pltpu.make_async_copy(ref, target, copied.at[j])
        for j, (ref, target) in enumerate(((norm_ref, norms), (grad_ref, grads), (shared_ref, outs)))
    ]
    for copy in copies:
        copy.start()
    for copy in copies:
        copy.wait()
    norm = norms[...].astype(F32)
    gate = gate_ref[...].astype(F32)
    gate_value = jax.nn.sigmoid(jnp.sum(norm * gate, axis=1, keepdims=True))
    inner = jnp.sum(grads[...].astype(F32) * outs[...].astype(F32), axis=1, keepdims=True)
    delta = inner * gate_value * (1.0 - gate_value)
    term_ref[...] = delta * gate
    local = jnp.sum(delta * norm, axis=0, keepdims=True)
    tail_ref[...] = jnp.zeros_like(tail_ref)
    for r in range(features // LANES):
        tail_ref[r : r + 1, :] = local[:, r * LANES : (r + 1) * LANES]


def shared(norm_input, out_grad, shared_out, shared_gate):
    tokens, features = norm_input.shape
    away = pl.BlockSpec(memory_space=pltpu.HBM)
    near = pl.BlockSpec(memory_space=pltpu.VMEM)
    return pl.pallas_call(
        shared_kernel,
        in_specs=[away, away, away, near],
        out_specs=[near, near],
        out_shape=[
            jax.ShapeDtypeStruct((tokens, LANES), F32),
            jax.ShapeDtypeStruct((tokens, features), F32),
        ],
        scratch_shapes=[pltpu.SemaphoreType.DMA((3,))]
        + [pltpu.VMEM((tokens, features), BF16)] * 3,
        compiler_params=pltpu.CompilerParams(vmem_limit_bytes=4 << 20),
        name="shared",
    )(*map(in_hbm, (norm_input, out_grad, shared_out)), shared_gate[None, :])


def finish_kernel(total_ref, *refs):
    parts, (term_ref, input_ref, route_ref, gate_ref) = refs[:-4], refs[-4:]
    tokens, features = term_ref.shape
    final = total_ref[:tokens].astype(F32)
    for part in parts:
        final = final + part[:tokens].astype(F32)
    input_ref[...] = (final[:, :features] + term_ref[...]).astype(BF16)
    line = features // LANES
    gate_ref[...] = final[:line, features:]
    lane = lax.broadcasted_iota(jnp.int32, (tokens, LANES), 1)
    token = lax.broadcasted_iota(jnp.int32, (tokens, LANES), 0)
    spread = jnp.where(lane // TOPK == token, final[line : line + 1, features:], 0.0)
    choose = (
        lax.broadcasted_iota(jnp.int32, (TOPK, LANES), 1) % TOPK
        == lax.broadcasted_iota(jnp.int32, (TOPK, LANES), 0)
    ).astype(F32)
    route_ref[...] = lax.dot_general(
        choose, spread, NT, precision=lax.Precision.HIGHEST, preferred_element_type=F32
    )


def finish(total, parts, term):
    tokens, features = term.shape
    return pl.pallas_call(
        finish_kernel,
        out_shape=[
            jax.ShapeDtypeStruct((tokens, features), BF16),
            jax.ShapeDtypeStruct((TOPK, tokens), F32),
            jax.ShapeDtypeStruct((features // LANES, LANES), F32),
        ],
        compiler_params=pltpu.CompilerParams(vmem_limit_bytes=4 << 20),
        name="finish",
    )(total, *parts, term)


def add(a, b):
    return (a.astype(F32) + b.astype(F32)).astype(BF16)


def square_device(
    norm_input, out_grad, shared_out, expert_ids, route_weight, shared_gate, w_gate, w_up, w_down
):
    tokens, features = norm_input.shape
    sources = lax.axis_size("expert")
    mine = pack(norm_input, out_grad, expert_ids, route_weight)
    tail, term = shared(norm_input, out_grad, shared_out, shared_gate)
    x0 = swap(mine, "dp", 2)
    z1 = swap(mine, "expert", 1)
    z2 = swap(mine, "expert", 2)
    z3 = swap(z2, "expert", 1)
    z3, tail, term = lax.optimization_barrier((z3, tail, term))
    xz1 = swap(z1, "dp", 2)
    xz2 = swap(z2, "dp", 2)
    xz3 = swap(xz2, "expert", 1)
    held = [mine, z1, z2, z3, x0, xz1, xz2, xz3]
    held = held + [swap(block, "dp", 1) for block in held]
    kept, sent = run_experts(held, tail, w_gate, w_up, w_down, sources)
    total = (kept.astype(F32) + swap(sent, "dp", 1).astype(F32)).astype(BF16)
    own = [total[j * tokens : (j + 1) * tokens] for j in range(2 * sources)]
    far = swap(jnp.concatenate([own[3], own[7]], axis=0), "expert", 1)
    near = swap(total[4 * tokens : 6 * tokens], "dp", 2)
    third = swap(add(own[6], far[tokens:]), "dp", 2)
    second = swap(add(own[1], near[tokens:]), "expert", 1)
    fourth = swap(add(add(own[2], far[:tokens]), third), "expert", 2)
    parts = [near, second, fourth]
    input_grad, route_grad, gate_grad = finish(total, parts, term)
    return (input_grad, route_grad.T, gate_grad.reshape(features))


def solution(mesh):
    square = mesh.shape["expert"] == 4 and mesh.shape["dp"] == 4
    on_device = square_device if square else general_device
    return jax.shard_map(
        on_device,
        mesh=mesh,
        in_specs=(
            P(("groups", "expert", "dp"), None),
            P(("groups", "expert", "dp"), None),
            P(("groups", "expert", "dp"), None),
            P(("groups", "expert", "dp"), None),
            P(("groups", "expert", "dp"), None),
            P(),
            P("expert", None, "dp"),
            P("expert", None, "dp"),
            P("expert", "dp", None),
        ),
        out_specs=(
            P(("groups", "expert", "dp"), None),
            P(("groups", "expert", "dp"), None),
            P("groups"),
        ),
        check_vma=False,
    )
```

```python
import functools

import jax
import jax.numpy as jnp
import numpy as np
from jax import lax
from jax.experimental import pallas as pl
from jax.experimental.pallas import tpu as pltpu
from jax.sharding import PartitionSpec as P

EXPERTS = 64
TOPK = 8
CAP = 12
LANES = 128
BF16 = jnp.bfloat16
F32 = jnp.float32
NT = (((1,), (1,)), ((), ()))
TN = (((0,), (0,)), ((), ()))


def slot_targets(group_ids):
    flat_ids = group_ids.reshape(-1)
    one_hot = (flat_ids[:, None] == jnp.arange(EXPERTS, dtype=jnp.int32)[None, :]).astype(jnp.int32)
    before = jnp.cumsum(one_hot, axis=0) - one_hot
    position = jnp.sum(before * one_hot, axis=1)
    return flat_ids * CAP + position


def general_device(
    norm_input, out_grad, shared_out, expert_ids, route_weight, shared_gate, w_gate, w_up, w_down
):
    features = norm_input.shape[1]
    group_norm, group_grad, group_codes, group_weight = (
        lax.all_gather(norm_input, "dp", axis=0, tiled=True),
        lax.all_gather(out_grad, "dp", axis=0, tiled=True),
        lax.all_gather(expert_ids.astype(jnp.bfloat16), "dp", axis=0, tiled=True),
        lax.all_gather(route_weight, "dp", axis=0, tiled=True),
    )
    group_ids = group_codes.astype(jnp.int32)
    group_tokens = group_norm.shape[0]
    target = slot_targets(group_ids)
    slots = jnp.arange(EXPERTS * CAP, dtype=jnp.int32)
    hits = (target[None, :] == slots[:, None]).astype(jnp.bfloat16)
    dispatch = hits.reshape(EXPERTS * CAP, group_tokens, TOPK).sum(axis=2)
    slot_norm = jnp.dot(dispatch, group_norm, preferred_element_type=jnp.float32).astype(
        jnp.bfloat16
    )
    slot_grad = jnp.dot(dispatch, group_grad, preferred_element_type=jnp.float32).astype(
        jnp.bfloat16
    )
    slot_norm = slot_norm.reshape(EXPERTS, CAP, features)
    slot_grad = slot_grad.reshape(EXPERTS, CAP, features)
    local_experts = w_gate.shape[0]
    quarter = CAP // lax.axis_size("dp")
    offset = lax.axis_index("dp") * quarter
    norm_share = lax.dynamic_slice_in_dim(slot_norm, offset, quarter, 1)
    grad_share = lax.dynamic_slice_in_dim(slot_grad, offset, quarter, 1)
    arrived_norm, arrived_grad = (
        lax.all_to_all(norm_share, "expert", split_axis=0, concat_axis=0, tiled=True),
        lax.all_to_all(grad_share, "expert", split_axis=0, concat_axis=0, tiled=True),
    )
    rows_in = lax.all_gather(arrived_norm, "dp", axis=1, tiled=True)
    grads_in = lax.all_gather(arrived_grad, "dp", axis=1, tiled=True)
    item_count = rows_in.shape[1]
    sources = rows_in.shape[0] // local_experts
    rows_four = rows_in.reshape(sources, local_experts, item_count, features)
    grads_four = grads_in.reshape(sources, local_experts, item_count, features)
    gate_pre = jnp.einsum("sxcd,xdf->sxcf", rows_four, w_gate, preferred_element_type=jnp.float32)
    up_pre = jnp.einsum("sxcd,xdf->sxcf", rows_four, w_up, preferred_element_type=jnp.float32)
    hidden_grad = jnp.einsum(
        "sxcd,xfd->sxcf", grads_four, w_down, preferred_element_type=jnp.float32
    )
    logistic = jax.nn.sigmoid(gate_pre)
    swish = gate_pre * logistic
    act = swish * up_pre
    gate_diff = (hidden_grad * up_pre * logistic * (1.0 + gate_pre * (1.0 - logistic))).astype(
        jnp.bfloat16
    )
    up_diff = (hidden_grad * swish).astype(jnp.bfloat16)
    row_part = jnp.einsum("sxcf,xdf->sxcd", gate_diff, w_gate, preferred_element_type=jnp.float32)
    row_part = row_part + jnp.einsum(
        "sxcf,xdf->sxcd", up_diff, w_up, preferred_element_type=jnp.float32
    )
    row_back = row_part.astype(jnp.bfloat16).reshape(sources * local_experts, item_count, features)
    score_back = jnp.sum(act * hidden_grad, axis=3).astype(jnp.bfloat16)
    score_back = score_back.reshape(sources * local_experts, item_count, 1)
    back_rows = lax.all_to_all(row_back, "expert", split_axis=0, concat_axis=0, tiled=True)
    back_scores = lax.all_to_all(score_back, "expert", split_axis=0, concat_axis=0, tiled=True)
    columns = back_rows.shape[2]
    back_flat = back_rows.reshape(EXPERTS * CAP, columns)
    score_flat = back_scores.reshape(EXPERTS * CAP)
    picked = jnp.take(back_flat, target, axis=0).reshape(group_tokens, TOPK, columns)
    token_part = jnp.einsum(
        "tk,tkd->td", group_weight.astype(jnp.float32), picked.astype(jnp.float32)
    )
    score_part = (
        jnp.take(score_flat, target, axis=0).astype(jnp.float32).reshape(group_tokens, TOPK)
    )
    routed, route_grad = (
        lax.psum_scatter(
            token_part.astype(jnp.bfloat16), "dp", scatter_dimension=0, tiled=True
        ).astype(jnp.float32),
        lax.psum_scatter(
            score_part.astype(jnp.bfloat16), "dp", scatter_dimension=0, tiled=True
        ).astype(jnp.float32),
    )
    gate_value = jax.nn.sigmoid(
        jnp.dot(norm_input, shared_gate, preferred_element_type=jnp.float32)
    )
    inner = jnp.sum(out_grad.astype(jnp.float32) * shared_out.astype(jnp.float32), axis=1)
    gate_delta = inner * gate_value * (1.0 - gate_value)
    input_grad = (routed + gate_delta[:, None] * shared_gate.astype(jnp.float32)[None, :]).astype(
        jnp.bfloat16
    )
    gate_local = jnp.dot(
        gate_delta, norm_input.astype(jnp.float32), precision=lax.Precision.HIGHEST
    )
    gate_grad = lax.psum(gate_local, ("expert", "dp"))
    return (input_grad, route_grad, gate_grad)


def dot(a, b, dims=(((1,), (0,)), ((), ()))):
    return lax.dot_general(a, b, dims, preferred_element_type=F32)


def swap(value, axis, distance):
    size = lax.axis_size(axis)
    return lax.ppermute(value, axis, [(i, i ^ distance) for i in range(size)])


def experts_kernel(features, rows, blocks, group, *refs):
    token_refs, refs = refs[:blocks], refs[blocks:]
    tail_ref, w_gate, w_up, w_down, keep_ref, send_ref, gates, ups, downs, loaded, spread, weighted, norms, grads, backs, hits, routes = refs
    number = w_gate.shape[0]
    starts = np.cumsum([0] + [ref.shape[0] for ref in token_refs])
    count = int(starts[-1])

    def loads(turn, k):
        expert = turn * group + k
        slot = lax.rem(turn, 3) * group + k
        return [
            pltpu.make_async_copy(source.at[expert], target.at[slot], loaded.at[slot, j])
            for j, (source, target) in enumerate(((w_gate, gates), (w_up, ups), (w_down, downs)))
        ]

    for k in range(group):
        for copy in loads(0, k):
            copy.start()
    def together(columns):
        return jnp.concatenate([ref[:, columns] for ref in token_refs], axis=0)

    codes = together(slice(2 * features, None)).astype(F32).T
    weights = codes[TOPK : 2 * TOPK]
    local = codes[:TOPK] - (lax.axis_index("expert") * number).astype(F32)
    hits[...] = local
    earlier = (
        lax.broadcasted_iota(jnp.int32, (count, count), 0)
        < lax.broadcasted_iota(jnp.int32, (count, count), 1)
    ).astype(BF16)
    masks = [local == float(e) for e in range(number)]
    member = jnp.concatenate(
        [jnp.sum(m.astype(F32), axis=0, keepdims=True) for m in masks], axis=0
    )
    position = dot(member.astype(BF16), earlier)
    slot = lax.broadcasted_iota(jnp.int32, (rows, count), 0).astype(F32)
    for e in range(number):
        weight = jnp.sum(jnp.where(masks[e], weights, 0.0), axis=0, keepdims=True)
        chosen = (slot == position[e : e + 1]) & (member[e : e + 1] > 0.0)
        spread[e * rows : (e + 1) * rows] = jnp.where(chosen, 1.0, 0.0).astype(BF16)
        weighted[e * rows : (e + 1) * rows] = jnp.where(chosen, weight, 0.0).astype(BF16)
    for k in range(group):
        for copy in loads(1, k):
            copy.start()
    norms[...] = dot(spread[...], together(slice(0, features))).astype(BF16)
    grads[...] = dot(spread[...], together(slice(features, 2 * features))).astype(BF16)
    routes[...] = jnp.zeros_like(routes)

    def run(turn, _):
        base = lax.rem(turn, 3) * group
        heres = [
            pl.ds(pl.multiple_of((turn * group + k) * rows, rows), rows) for k in range(group)
        ]
        for k in range(group):
            for copy in loads(turn, k):
                copy.wait()
        @pl.when(turn + 2 < number // group)
        def _():
            for k in range(group):
                for copy in loads(turn + 2, k):
                    copy.start()

        pre = []
        for k in range(group):
            x, dy = norms[heres[k]], grads[heres[k]]
            pre.append((dot(x, gates[base + k]), dot(x, ups[base + k]), dot(dy, downs[base + k], NT)))
        for k in range(group):
            gate_pre, up_pre, hidden_grad = pre[k]
            logistic = jax.nn.sigmoid(gate_pre)
            swish = gate_pre * logistic
            gate_diff = (
                hidden_grad * up_pre * logistic * (1.0 + gate_pre * (1.0 - logistic))
            ).astype(BF16)
            up_diff = (hidden_grad * swish).astype(BF16)
            for left in range(0, features, 512):
                cut = slice(left, min(left + 512, features))
                first_part = dot(gate_diff, gates[base + k, cut], NT)
                second_part = dot(ups[base + k, cut], up_diff, NT).T
                backs[heres[k], cut] = (first_part + second_part).astype(BF16)
            score = jnp.sum(swish * up_pre * hidden_grad, axis=1, keepdims=True)
            by_token = jnp.sum(spread[heres[k]].astype(F32) * score, axis=0, keepdims=True)
            here = (turn * group + k).astype(F32)
            routes[...] += jnp.where(hits[...] == here, by_token, 0.0)

        return 0

    lax.fori_loop(0, number // group, run, 0)
    half = count // 2
    result = dot(weighted[...], backs[...], TN).astype(BF16)
    each = tail_ref.shape[0]
    line = features // LANES
    token = lax.broadcasted_iota(jnp.int32, (count, LANES), 0)
    lane = lax.broadcasted_iota(jnp.int32, (count, LANES), 1)
    repeat = (
        lax.broadcasted_iota(jnp.int32, (TOPK, LANES), 1) % TOPK
        == lax.broadcasted_iota(jnp.int32, (TOPK, LANES), 0)
    ).astype(BF16)
    scores = dot(routes[...].astype(BF16), repeat, TN)
    scores = jnp.where(lane // TOPK == token % each, scores, 0.0).astype(BF16)
    row = lax.broadcasted_iota(jnp.int32, (count, count), 0)
    column = lax.broadcasted_iota(jnp.int32, (count, count), 1)
    gather = ((row % each == line) & (row // each == column // each)).astype(BF16)
    tail = jnp.concatenate([tail_ref[...]] * (count // each), axis=0)
    last = (dot(gather, scores) + tail).astype(BF16)
    keep_ref[:, :features] = result[:half]
    send_ref[:, :features] = result[half:]
    keep_ref[:, features:] = last[:half]
    send_ref[:, features:] = last[half:]


def run_experts(token_blocks, tail, w_gate, w_up, w_down, sources):
    local, features, hidden = w_gate.shape
    blocks = len(token_blocks)
    count = sum(block.shape[0] for block in token_blocks)
    rows = sources * CAP
    width = features + LANES
    group = 2
    away = pl.BlockSpec(memory_space=pl.ANY)
    near = pl.BlockSpec(memory_space=pltpu.VMEM)
    return pl.pallas_call(
        functools.partial(experts_kernel, features, rows, blocks, group),
        in_specs=[near] * (blocks + 1) + [away] * 3,
        out_specs=[near] * 2,
        out_shape=[jax.ShapeDtypeStruct((count // 2, width), BF16)] * 2,
        scratch_shapes=[
            pltpu.VMEM((3 * group, features, hidden), BF16),
            pltpu.VMEM((3 * group, features, hidden), BF16),
            pltpu.VMEM((3 * group, hidden, features), BF16),
            pltpu.SemaphoreType.DMA((3 * group, 3)),
            pltpu.VMEM((local * rows, count), BF16),
            pltpu.VMEM((local * rows, count), BF16),
            pltpu.VMEM((local * rows, features), BF16),
            pltpu.VMEM((local * rows, features), BF16),
            pltpu.VMEM((local * rows, features), BF16),
            pltpu.VMEM((TOPK, count), F32),
            pltpu.VMEM((TOPK, count), F32),
        ],
        compiler_params=pltpu.CompilerParams(vmem_limit_bytes=44 << 20),
        name="experts",
    )(*token_blocks, tail, w_gate, w_up, w_down)


def in_hbm(value):
    return pltpu.with_memory_space_constraint(value, pltpu.HBM)


def pack_kernel(norm_ref, grad_ref, ids_ref, weight_ref, packed_ref, copied):
    features = norm_ref.shape[1]
    copies = [
        pltpu.make_async_copy(ref, packed_ref.at[:, pl.ds(j * features, features)], copied.at[j])
        for j, ref in enumerate((norm_ref, grad_ref))
    ]
    for copy in copies:
        copy.start()
    lane = lax.broadcasted_iota(jnp.int32, (TOPK, LANES), 1)
    source = lax.broadcasted_iota(jnp.int32, (TOPK, LANES), 0)
    ids = ids_ref[...].astype(F32).astype(BF16)
    codes = dot(ids, (lane == source).astype(BF16), TN) + dot(
        weight_ref[...], (lane == source + TOPK).astype(BF16), TN
    )
    packed_ref[:, 2 * features :] = codes.astype(BF16)
    for copy in copies:
        copy.wait()


def pack(norm_input, out_grad, expert_ids, route_weight):
    tokens, features = norm_input.shape
    away = pl.BlockSpec(memory_space=pltpu.HBM)
    near = pl.BlockSpec(memory_space=pltpu.VMEM)
    return pl.pallas_call(
        pack_kernel,
        in_specs=[away, away, near, near],
        out_specs=near,
        out_shape=jax.ShapeDtypeStruct((tokens, 2 * features + LANES), BF16),
        scratch_shapes=[pltpu.SemaphoreType.DMA((2,))],
        compiler_params=pltpu.CompilerParams(vmem_limit_bytes=4 << 20),
        name="pack",
    )(*map(in_hbm, (norm_input, out_grad, expert_ids.T, route_weight.T)))


def shared_kernel(norm_ref, grad_ref, shared_ref, gate_ref, tail_ref, term_ref, copied, norms, grads, outs):
    features = norm_ref.shape[1]
    copies = [
        pltpu.make_async_copy(ref, target, copied.at[j])
        for j, (ref, target) in enumerate(((norm_ref, norms), (grad_ref, grads), (shared_ref, outs)))
    ]
    for copy in copies:
        copy.start()
    for copy in copies:
        copy.wait()
    norm = norms[...].astype(F32)
    gate = gate_ref[...].astype(F32)
    gate_value = jax.nn.sigmoid(jnp.sum(norm * gate, axis=1, keepdims=True))
    inner = jnp.sum(grads[...].astype(F32) * outs[...].astype(F32), axis=1, keepdims=True)
    delta = inner * gate_value * (1.0 - gate_value)
    term_ref[...] = delta * gate
    local = jnp.sum(delta * norm, axis=0, keepdims=True)
    tail_ref[...] = jnp.zeros_like(tail_ref)
    for r in range(features // LANES):
        tail_ref[r : r + 1, :] = local[:, r * LANES : (r + 1) * LANES]


def shared(norm_input, out_grad, shared_out, shared_gate):
    tokens, features = norm_input.shape
    away = pl.BlockSpec(memory_space=pltpu.HBM)
    near = pl.BlockSpec(memory_space=pltpu.VMEM)
    return pl.pallas_call(
        shared_kernel,
        in_specs=[away, away, away, near],
        out_specs=[near, near],
        out_shape=[
            jax.ShapeDtypeStruct((tokens, LANES), F32),
            jax.ShapeDtypeStruct((tokens, features), F32),
        ],
        scratch_shapes=[pltpu.SemaphoreType.DMA((3,))]
        + [pltpu.VMEM((tokens, features), BF16)] * 3,
        compiler_params=pltpu.CompilerParams(vmem_limit_bytes=4 << 20),
        name="shared",
    )(*map(in_hbm, (norm_input, out_grad, shared_out)), shared_gate[None, :])


def finish_kernel(total_ref, *refs):
    parts, (term_ref, input_ref, route_ref, gate_ref) = refs[:-4], refs[-4:]
    tokens, features = term_ref.shape
    final = total_ref[:tokens].astype(F32)
    for part in parts:
        final = final + part[:tokens].astype(F32)
    input_ref[...] = (final[:, :features] + term_ref[...]).astype(BF16)
    line = features // LANES
    gate_ref[...] = final[:line, features:]
    lane = lax.broadcasted_iota(jnp.int32, (tokens, LANES), 1)
    token = lax.broadcasted_iota(jnp.int32, (tokens, LANES), 0)
    spread = jnp.where(lane // TOPK == token, final[line : line + 1, features:], 0.0)
    choose = (
        lax.broadcasted_iota(jnp.int32, (TOPK, LANES), 1) % TOPK
        == lax.broadcasted_iota(jnp.int32, (TOPK, LANES), 0)
    ).astype(F32)
    route_ref[...] = lax.dot_general(
        choose, spread, NT, precision=lax.Precision.HIGHEST, preferred_element_type=F32
    )


def finish(total, parts, term):
    tokens, features = term.shape
    return pl.pallas_call(
        finish_kernel,
        out_shape=[
            jax.ShapeDtypeStruct((tokens, features), BF16),
            jax.ShapeDtypeStruct((TOPK, tokens), F32),
            jax.ShapeDtypeStruct((features // LANES, LANES), F32),
        ],
        compiler_params=pltpu.CompilerParams(vmem_limit_bytes=4 << 20),
        name="finish",
    )(total, *parts, term)


def add(a, b):
    return (a.astype(F32) + b.astype(F32)).astype(BF16)


def square_device(
    norm_input, out_grad, shared_out, expert_ids, route_weight, shared_gate, w_gate, w_up, w_down
):
    tokens, features = norm_input.shape
    sources = lax.axis_size("expert")
    mine = pack(norm_input, out_grad, expert_ids, route_weight)
    tail, term = shared(norm_input, out_grad, shared_out, shared_gate)
    x0 = swap(mine, "dp", 2)
    z1 = swap(mine, "expert", 1)
    z2 = swap(mine, "expert", 2)
    z3 = swap(z2, "expert", 1)
    z3, tail, term = lax.optimization_barrier((z3, tail, term))
    xz1 = swap(z1, "dp", 2)
    xz2 = swap(z2, "dp", 2)
    xz3 = swap(xz2, "expert", 1)
    held = [mine, z1, z2, z3, x0, xz1, xz2, xz3]
    held = held + [swap(block, "dp", 1) for block in held]
    kept, sent = run_experts(held, tail, w_gate, w_up, w_down, sources)
    total = (kept.astype(F32) + swap(sent, "dp", 1).astype(F32)).astype(BF16)
    own = [total[j * tokens : (j + 1) * tokens] for j in range(2 * sources)]
    far = swap(jnp.concatenate([own[3], own[7]], axis=0), "expert", 1)
    near = swap(total[4 * tokens : 6 * tokens], "dp", 2)
    third = swap(add(own[6], far[tokens:]), "dp", 2)
    second = swap(add(own[1], near[tokens:]), "expert", 1)
    fourth = swap(add(add(own[2], far[:tokens]), third), "expert", 2)
    parts = [near, second, fourth]
    input_grad, route_grad, gate_grad = finish(total, parts, term)
    return (input_grad, route_grad.T, gate_grad.reshape(features))


def solution(mesh):
    square = mesh.shape["expert"] == 4 and mesh.shape["dp"] == 4
    on_device = square_device if square else general_device
    return jax.shard_map(
        on_device,
        mesh=mesh,
        in_specs=(
            P(("groups", "expert", "dp"), None),
            P(("groups", "expert", "dp"), None),
            P(("groups", "expert", "dp"), None),
            P(("groups", "expert", "dp"), None),
            P(("groups", "expert", "dp"), None),
            P(),
            P("expert", None, "dp"),
            P("expert", None, "dp"),
            P("expert", "dp", None),
        ),
        out_specs=(
            P(("groups", "expert", "dp"), None),
            P(("groups", "expert", "dp"), None),
            P("groups"),
        ),
        check_vma=False,
    )
```

```python
import functools

import jax
import jax.numpy as jnp
import numpy as np
from jax import lax
from jax.experimental import pallas as pl
from jax.experimental.pallas import tpu as pltpu
from jax.sharding import PartitionSpec as P

EXPERTS = 64
TOPK = 8
CAP = 12
LANES = 128
BF16 = jnp.bfloat16
F32 = jnp.float32
NT = (((1,), (1,)), ((), ()))
TN = (((0,), (0,)), ((), ()))


def slot_targets(group_ids):
    flat_ids = group_ids.reshape(-1)
    one_hot = (flat_ids[:, None] == jnp.arange(EXPERTS, dtype=jnp.int32)[None, :]).astype(jnp.int32)
    before = jnp.cumsum(one_hot, axis=0) - one_hot
    position = jnp.sum(before * one_hot, axis=1)
    return flat_ids * CAP + position


def general_device(
    norm_input, out_grad, shared_out, expert_ids, route_weight, shared_gate, w_gate, w_up, w_down
):
    features = norm_input.shape[1]
    group_norm, group_grad, group_codes, group_weight = (
        lax.all_gather(norm_input, "dp", axis=0, tiled=True),
        lax.all_gather(out_grad, "dp", axis=0, tiled=True),
        lax.all_gather(expert_ids.astype(jnp.bfloat16), "dp", axis=0, tiled=True),
        lax.all_gather(route_weight, "dp", axis=0, tiled=True),
    )
    group_ids = group_codes.astype(jnp.int32)
    group_tokens = group_norm.shape[0]
    target = slot_targets(group_ids)
    slots = jnp.arange(EXPERTS * CAP, dtype=jnp.int32)
    hits = (target[None, :] == slots[:, None]).astype(jnp.bfloat16)
    dispatch = hits.reshape(EXPERTS * CAP, group_tokens, TOPK).sum(axis=2)
    slot_norm = jnp.dot(dispatch, group_norm, preferred_element_type=jnp.float32).astype(
        jnp.bfloat16
    )
    slot_grad = jnp.dot(dispatch, group_grad, preferred_element_type=jnp.float32).astype(
        jnp.bfloat16
    )
    slot_norm = slot_norm.reshape(EXPERTS, CAP, features)
    slot_grad = slot_grad.reshape(EXPERTS, CAP, features)
    local_experts = w_gate.shape[0]
    quarter = CAP // lax.axis_size("dp")
    offset = lax.axis_index("dp") * quarter
    norm_share = lax.dynamic_slice_in_dim(slot_norm, offset, quarter, 1)
    grad_share = lax.dynamic_slice_in_dim(slot_grad, offset, quarter, 1)
    arrived_norm, arrived_grad = (
        lax.all_to_all(norm_share, "expert", split_axis=0, concat_axis=0, tiled=True),
        lax.all_to_all(grad_share, "expert", split_axis=0, concat_axis=0, tiled=True),
    )
    rows_in = lax.all_gather(arrived_norm, "dp", axis=1, tiled=True)
    grads_in = lax.all_gather(arrived_grad, "dp", axis=1, tiled=True)
    item_count = rows_in.shape[1]
    sources = rows_in.shape[0] // local_experts
    rows_four = rows_in.reshape(sources, local_experts, item_count, features)
    grads_four = grads_in.reshape(sources, local_experts, item_count, features)
    gate_pre = jnp.einsum("sxcd,xdf->sxcf", rows_four, w_gate, preferred_element_type=jnp.float32)
    up_pre = jnp.einsum("sxcd,xdf->sxcf", rows_four, w_up, preferred_element_type=jnp.float32)
    hidden_grad = jnp.einsum(
        "sxcd,xfd->sxcf", grads_four, w_down, preferred_element_type=jnp.float32
    )
    logistic = jax.nn.sigmoid(gate_pre)
    swish = gate_pre * logistic
    act = swish * up_pre
    gate_diff = (hidden_grad * up_pre * logistic * (1.0 + gate_pre * (1.0 - logistic))).astype(
        jnp.bfloat16
    )
    up_diff = (hidden_grad * swish).astype(jnp.bfloat16)
    row_part = jnp.einsum("sxcf,xdf->sxcd", gate_diff, w_gate, preferred_element_type=jnp.float32)
    row_part = row_part + jnp.einsum(
        "sxcf,xdf->sxcd", up_diff, w_up, preferred_element_type=jnp.float32
    )
    row_back = row_part.astype(jnp.bfloat16).reshape(sources * local_experts, item_count, features)
    score_back = jnp.sum(act * hidden_grad, axis=3).astype(jnp.bfloat16)
    score_back = score_back.reshape(sources * local_experts, item_count, 1)
    back_rows = lax.all_to_all(row_back, "expert", split_axis=0, concat_axis=0, tiled=True)
    back_scores = lax.all_to_all(score_back, "expert", split_axis=0, concat_axis=0, tiled=True)
    columns = back_rows.shape[2]
    back_flat = back_rows.reshape(EXPERTS * CAP, columns)
    score_flat = back_scores.reshape(EXPERTS * CAP)
    picked = jnp.take(back_flat, target, axis=0).reshape(group_tokens, TOPK, columns)
    token_part = jnp.einsum(
        "tk,tkd->td", group_weight.astype(jnp.float32), picked.astype(jnp.float32)
    )
    score_part = (
        jnp.take(score_flat, target, axis=0).astype(jnp.float32).reshape(group_tokens, TOPK)
    )
    routed, route_grad = (
        lax.psum_scatter(
            token_part.astype(jnp.bfloat16), "dp", scatter_dimension=0, tiled=True
        ).astype(jnp.float32),
        lax.psum_scatter(
            score_part.astype(jnp.bfloat16), "dp", scatter_dimension=0, tiled=True
        ).astype(jnp.float32),
    )
    gate_value = jax.nn.sigmoid(
        jnp.dot(norm_input, shared_gate, preferred_element_type=jnp.float32)
    )
    inner = jnp.sum(out_grad.astype(jnp.float32) * shared_out.astype(jnp.float32), axis=1)
    gate_delta = inner * gate_value * (1.0 - gate_value)
    input_grad = (routed + gate_delta[:, None] * shared_gate.astype(jnp.float32)[None, :]).astype(
        jnp.bfloat16
    )
    gate_local = jnp.dot(
        gate_delta, norm_input.astype(jnp.float32), precision=lax.Precision.HIGHEST
    )
    gate_grad = lax.psum(gate_local, ("expert", "dp"))
    return (input_grad, route_grad, gate_grad)


def dot(a, b, dims=(((1,), (0,)), ((), ()))):
    return lax.dot_general(a, b, dims, preferred_element_type=F32)


def swap(value, axis, distance):
    size = lax.axis_size(axis)
    return lax.ppermute(value, axis, [(i, i ^ distance) for i in range(size)])


def experts_kernel(features, rows, blocks, group, *refs):
    token_refs, refs = refs[:blocks], refs[blocks:]
    tail_ref, w_gate, w_up, w_down, keep_ref, send_ref, gates, ups, downs, loaded, spread, weighted, norms, grads, backs, hits, routes = refs
    number = w_gate.shape[0]
    starts = np.cumsum([0] + [ref.shape[0] for ref in token_refs])
    count = int(starts[-1])

    def loads(turn, k):
        expert = turn * group + k
        slot = lax.rem(turn, 3) * group + k
        return [
            pltpu.make_async_copy(source.at[expert], target.at[slot], loaded.at[slot, j])
            for j, (source, target) in enumerate(((w_gate, gates), (w_up, ups), (w_down, downs)))
        ]

    for k in range(group):
        for copy in loads(0, k):
            copy.start()
    def together(columns):
        return jnp.concatenate([ref[:, columns] for ref in token_refs], axis=0)

    codes = together(slice(2 * features, None)).astype(F32).T
    weights = codes[TOPK : 2 * TOPK]
    local = codes[:TOPK] - (lax.axis_index("expert") * number).astype(F32)
    hits[...] = local
    earlier = (
        lax.broadcasted_iota(jnp.int32, (count, count), 0)
        < lax.broadcasted_iota(jnp.int32, (count, count), 1)
    ).astype(BF16)
    masks = [local == float(e) for e in range(number)]
    member = jnp.concatenate(
        [jnp.sum(m.astype(F32), axis=0, keepdims=True) for m in masks], axis=0
    )
    position = dot(member.astype(BF16), earlier)
    slot = lax.broadcasted_iota(jnp.int32, (rows, count), 0).astype(F32)
    for e in range(number):
        weight = jnp.sum(jnp.where(masks[e], weights, 0.0), axis=0, keepdims=True)
        chosen = (slot == position[e : e + 1]) & (member[e : e + 1] > 0.0)
        spread[e * rows : (e + 1) * rows] = jnp.where(chosen, 1.0, 0.0).astype(BF16)
        weighted[e * rows : (e + 1) * rows] = jnp.where(chosen, weight, 0.0).astype(BF16)
    for k in range(group):
        for copy in loads(1, k):
            copy.start()
    for target, first in ((norms, 0), (grads, features)):
        for left in range(0, features, 512):
            right = min(left + 512, features)
            piece = together(slice(first + left, first + right))
            target[:, left:right] = dot(spread[...], piece).astype(BF16)
    routes[...] = jnp.zeros_like(routes)

    def run(turn, _):
        base = lax.rem(turn, 3) * group
        heres = [
            pl.ds(pl.multiple_of((turn * group + k) * rows, rows), rows) for k in range(group)
        ]
        for k in range(group):
            for copy in loads(turn, k):
                copy.wait()
        @pl.when(turn + 2 < number // group)
        def _():
            for k in range(group):
                for copy in loads(turn + 2, k):
                    copy.start()

        pre = []
        for k in range(group):
            x, dy = norms[heres[k]], grads[heres[k]]
            pre.append((dot(x, gates[base + k]), dot(x, ups[base + k]), dot(dy, downs[base + k], NT)))
        for k in range(group):
            gate_pre, up_pre, hidden_grad = pre[k]
            logistic = jax.nn.sigmoid(gate_pre)
            swish = gate_pre * logistic
            gate_diff = (
                hidden_grad * up_pre * logistic * (1.0 + gate_pre * (1.0 - logistic))
            ).astype(BF16)
            up_diff = (hidden_grad * swish).astype(BF16)
            for left in range(0, features, 512):
                cut = slice(left, min(left + 512, features))
                first_part = dot(gate_diff, gates[base + k, cut], NT)
                second_part = dot(ups[base + k, cut], up_diff, NT).T
                backs[heres[k], cut] = (first_part + second_part).astype(BF16)
            score = jnp.sum(swish * up_pre * hidden_grad, axis=1, keepdims=True)
            by_token = jnp.sum(spread[heres[k]].astype(F32) * score, axis=0, keepdims=True)
            here = (turn * group + k).astype(F32)
            routes[...] += jnp.where(hits[...] == here, by_token, 0.0)

        return 0

    lax.fori_loop(0, number // group, run, 0)
    half = count // 2
    result = dot(weighted[...], backs[...], TN).astype(BF16)
    each = tail_ref.shape[0]
    line = features // LANES
    token = lax.broadcasted_iota(jnp.int32, (count, LANES), 0)
    lane = lax.broadcasted_iota(jnp.int32, (count, LANES), 1)
    repeat = (
        lax.broadcasted_iota(jnp.int32, (TOPK, LANES), 1) % TOPK
        == lax.broadcasted_iota(jnp.int32, (TOPK, LANES), 0)
    ).astype(BF16)
    scores = dot(routes[...].astype(BF16), repeat, TN)
    scores = jnp.where(lane // TOPK == token % each, scores, 0.0).astype(BF16)
    row = lax.broadcasted_iota(jnp.int32, (count, count), 0)
    column = lax.broadcasted_iota(jnp.int32, (count, count), 1)
    gather = ((row % each == line) & (row // each == column // each)).astype(BF16)
    tail = jnp.concatenate([tail_ref[...]] * (count // each), axis=0)
    last = (dot(gather, scores) + tail).astype(BF16)
    keep_ref[:, :features] = result[:half]
    send_ref[:, :features] = result[half:]
    keep_ref[:, features:] = last[:half]
    send_ref[:, features:] = last[half:]


def run_experts(token_blocks, tail, w_gate, w_up, w_down, sources):
    local, features, hidden = w_gate.shape
    blocks = len(token_blocks)
    count = sum(block.shape[0] for block in token_blocks)
    rows = sources * CAP
    width = features + LANES
    group = 2
    away = pl.BlockSpec(memory_space=pl.ANY)
    near = pl.BlockSpec(memory_space=pltpu.VMEM)
    return pl.pallas_call(
        functools.partial(experts_kernel, features, rows, blocks, group),
        in_specs=[near] * (blocks + 1) + [away] * 3,
        out_specs=[near] * 2,
        out_shape=[jax.ShapeDtypeStruct((count // 2, width), BF16)] * 2,
        scratch_shapes=[
            pltpu.VMEM((3 * group, features, hidden), BF16),
            pltpu.VMEM((3 * group, features, hidden), BF16),
            pltpu.VMEM((3 * group, hidden, features), BF16),
            pltpu.SemaphoreType.DMA((3 * group, 3)),
            pltpu.VMEM((local * rows, count), BF16),
            pltpu.VMEM((local * rows, count), BF16),
            pltpu.VMEM((local * rows, features), BF16),
            pltpu.VMEM((local * rows, features), BF16),
            pltpu.VMEM((local * rows, features), BF16),
            pltpu.VMEM((TOPK, count), F32),
            pltpu.VMEM((TOPK, count), F32),
        ],
        compiler_params=pltpu.CompilerParams(vmem_limit_bytes=44 << 20),
        name="experts",
    )(*token_blocks, tail, w_gate, w_up, w_down)


def in_hbm(value):
    return pltpu.with_memory_space_constraint(value, pltpu.HBM)


def pack_kernel(norm_ref, grad_ref, ids_ref, weight_ref, packed_ref, copied):
    features = norm_ref.shape[1]
    copies = [
        pltpu.make_async_copy(ref, packed_ref.at[:, pl.ds(j * features, features)], copied.at[j])
        for j, ref in enumerate((norm_ref, grad_ref))
    ]
    for copy in copies:
        copy.start()
    lane = lax.broadcasted_iota(jnp.int32, (TOPK, LANES), 1)
    source = lax.broadcasted_iota(jnp.int32, (TOPK, LANES), 0)
    ids = ids_ref[...].astype(F32).astype(BF16)
    codes = dot(ids, (lane == source).astype(BF16), TN) + dot(
        weight_ref[...], (lane == source + TOPK).astype(BF16), TN
    )
    packed_ref[:, 2 * features :] = codes.astype(BF16)
    for copy in copies:
        copy.wait()


def pack(norm_input, out_grad, expert_ids, route_weight):
    tokens, features = norm_input.shape
    away = pl.BlockSpec(memory_space=pltpu.HBM)
    near = pl.BlockSpec(memory_space=pltpu.VMEM)
    return pl.pallas_call(
        pack_kernel,
        in_specs=[away, away, near, near],
        out_specs=near,
        out_shape=jax.ShapeDtypeStruct((tokens, 2 * features + LANES), BF16),
        scratch_shapes=[pltpu.SemaphoreType.DMA((2,))],
        compiler_params=pltpu.CompilerParams(vmem_limit_bytes=4 << 20),
        name="pack",
    )(*map(in_hbm, (norm_input, out_grad, expert_ids.T, route_weight.T)))


def shared_kernel(norm_ref, grad_ref, shared_ref, gate_ref, tail_ref, term_ref, copied, norms, grads, outs):
    features = norm_ref.shape[1]
    copies = [
        pltpu.make_async_copy(ref, target, copied.at[j])
        for j, (ref, target) in enumerate(((norm_ref, norms), (grad_ref, grads), (shared_ref, outs)))
    ]
    for copy in copies:
        copy.start()
    for copy in copies:
        copy.wait()
    norm = norms[...].astype(F32)
    gate = gate_ref[...].astype(F32)
    gate_value = jax.nn.sigmoid(jnp.sum(norm * gate, axis=1, keepdims=True))
    inner = jnp.sum(grads[...].astype(F32) * outs[...].astype(F32), axis=1, keepdims=True)
    delta = inner * gate_value * (1.0 - gate_value)
    term_ref[...] = delta * gate
    local = jnp.sum(delta * norm, axis=0, keepdims=True)
    tail_ref[...] = jnp.zeros_like(tail_ref)
    for r in range(features // LANES):
        tail_ref[r : r + 1, :] = local[:, r * LANES : (r + 1) * LANES]


def shared(norm_input, out_grad, shared_out, shared_gate):
    tokens, features = norm_input.shape
    away = pl.BlockSpec(memory_space=pltpu.HBM)
    near = pl.BlockSpec(memory_space=pltpu.VMEM)
    return pl.pallas_call(
        shared_kernel,
        in_specs=[away, away, away, near],
        out_specs=[near, near],
        out_shape=[
            jax.ShapeDtypeStruct((tokens, LANES), F32),
            jax.ShapeDtypeStruct((tokens, features), F32),
        ],
        scratch_shapes=[pltpu.SemaphoreType.DMA((3,))]
        + [pltpu.VMEM((tokens, features), BF16)] * 3,
        compiler_params=pltpu.CompilerParams(vmem_limit_bytes=4 << 20),
        name="shared",
    )(*map(in_hbm, (norm_input, out_grad, shared_out)), shared_gate[None, :])


def finish_kernel(total_ref, *refs):
    parts, (term_ref, input_ref, route_ref, gate_ref) = refs[:-4], refs[-4:]
    tokens, features = term_ref.shape
    final = total_ref[:tokens].astype(F32)
    for part in parts:
        final = final + part[:tokens].astype(F32)
    input_ref[...] = (final[:, :features] + term_ref[...]).astype(BF16)
    line = features // LANES
    gate_ref[...] = final[:line, features:]
    lane = lax.broadcasted_iota(jnp.int32, (tokens, LANES), 1)
    token = lax.broadcasted_iota(jnp.int32, (tokens, LANES), 0)
    spread = jnp.where(lane // TOPK == token, final[line : line + 1, features:], 0.0)
    choose = (
        lax.broadcasted_iota(jnp.int32, (TOPK, LANES), 1) % TOPK
        == lax.broadcasted_iota(jnp.int32, (TOPK, LANES), 0)
    ).astype(F32)
    route_ref[...] = lax.dot_general(
        choose, spread, NT, precision=lax.Precision.HIGHEST, preferred_element_type=F32
    )


def finish(total, parts, term):
    tokens, features = term.shape
    return pl.pallas_call(
        finish_kernel,
        out_shape=[
            jax.ShapeDtypeStruct((tokens, features), BF16),
            jax.ShapeDtypeStruct((TOPK, tokens), F32),
            jax.ShapeDtypeStruct((features // LANES, LANES), F32),
        ],
        compiler_params=pltpu.CompilerParams(vmem_limit_bytes=4 << 20),
        name="finish",
    )(total, *parts, term)


def add(a, b):
    return (a.astype(F32) + b.astype(F32)).astype(BF16)


def square_device(
    norm_input, out_grad, shared_out, expert_ids, route_weight, shared_gate, w_gate, w_up, w_down
):
    tokens, features = norm_input.shape
    sources = lax.axis_size("expert")
    mine = pack(norm_input, out_grad, expert_ids, route_weight)
    tail, term = shared(norm_input, out_grad, shared_out, shared_gate)
    x0 = swap(mine, "dp", 2)
    z1 = swap(mine, "expert", 1)
    z2 = swap(mine, "expert", 2)
    z3 = swap(z2, "expert", 1)
    z3, tail, term = lax.optimization_barrier((z3, tail, term))
    xz1 = swap(z1, "dp", 2)
    xz2 = swap(z2, "dp", 2)
    xz3 = swap(xz2, "expert", 1)
    held = [mine, z1, z2, z3, x0, xz1, xz2, xz3]
    held = held + [swap(block, "dp", 1) for block in held]
    kept, sent = run_experts(held, tail, w_gate, w_up, w_down, sources)
    total = (kept.astype(F32) + swap(sent, "dp", 1).astype(F32)).astype(BF16)
    own = [total[j * tokens : (j + 1) * tokens] for j in range(2 * sources)]
    far = swap(jnp.concatenate([own[3], own[7]], axis=0), "expert", 1)
    near = swap(total[4 * tokens : 6 * tokens], "dp", 2)
    third = swap(add(own[6], far[tokens:]), "dp", 2)
    second = swap(add(own[1], near[tokens:]), "expert", 1)
    fourth = swap(add(add(own[2], far[:tokens]), third), "expert", 2)
    parts = [near, second, fourth]
    input_grad, route_grad, gate_grad = finish(total, parts, term)
    return (input_grad, route_grad.T, gate_grad.reshape(features))


def solution(mesh):
    square = mesh.shape["expert"] == 4 and mesh.shape["dp"] == 4
    on_device = square_device if square else general_device
    return jax.shard_map(
        on_device,
        mesh=mesh,
        in_specs=(
            P(("groups", "expert", "dp"), None),
            P(("groups", "expert", "dp"), None),
            P(("groups", "expert", "dp"), None),
            P(("groups", "expert", "dp"), None),
            P(("groups", "expert", "dp"), None),
            P(),
            P("expert", None, "dp"),
            P("expert", None, "dp"),
            P("expert", "dp", None),
        ),
        out_specs=(
            P(("groups", "expert", "dp"), None),
            P(("groups", "expert", "dp"), None),
            P("groups"),
        ),
        check_vma=False,
    )
```
